256 devices in a mesh: blk: 8 (over y, core), kvh: 4 (over z_lo), dec: 8 (over x, z_hi).
Axes of the slice: x: 4, y: 4, z: 8 (z_hi: 2, z_lo: 4; z = z_hi * 4 + z_lo), core: 2. Of those that a mesh axis runs over, the one named last changes fastest.
Arguments:
- queries: bfloat16 [8192, 8192], P('blk', ('kvh', 'dec')), may hold values from -6 to 6
- keys: bfloat16 [8192, 1024], P(('blk', 'dec'), 'kvh'), may hold values from -6 to 6
- values: bfloat16 [8192, 1024], P(('blk', 'dec'), 'kvh'), may hold values from -6 to 6
- page_slot: int32 [64], replicated, may hold values from 0 to 127, as said below
Outputs:
- attended: bfloat16 [8192, 8192], P('blk', ('kvh', 'dec'))
- cache_keys: bfloat16 [16384, 1024], P(('blk', 'dec'), 'kvh')
- cache_values: bfloat16 [16384, 1024], P(('blk', 'dec'), 'kvh')
- key_scales: float32 [128, 8], P(('blk', 'dec'), 'kvh')
- value_scales: float32 [128, 8], P(('blk', 'dec'), 'kvh')
The draws below stay inside these ranges and needn't reach their ends.
Inputs may be any that keep to these rules, and one draw needn't show every extreme that they name: `page_slot`: the values are distinct; slot s belongs to decode owner s // 2 (its index along blk+dec) as its slot s % 2.
All inputs are finite; a program needn't handle non-finite values. Where the reference program divides by a largest or mean magnitude, that divisor is 1e-20 or more.
Results may differ from the reference program's by a relative error of at most 0.0045.
Values may be sent and summed in bfloat16 or wider, within the bound.
No kernel may reach another device: no remote copies, remote signals or barrier semaphores. Data moves between devices by JAX's collectives and lax.ppermute only.
A program may use at most 256 MiB of HBM per device.

```python
import jax
import jax.numpy as jnp
from jax import lax

HEADS = 64
KVH = 8
HD = 128
PAGE = 128
TOKENS = 8192
SLOTS = 2
OWNERS = 64
PAGES = 64


def draw_queries(key, part):
    key = jax.random.fold_in(key, 11)
    base = jnp.clip(jax.random.normal(key, (TOKENS, HEADS * HD), jnp.float32), -6.0, 6.0)
    return base.astype(jnp.bfloat16)


def draw_keys(key, part):
    key = jax.random.fold_in(key, 23)
    base = jnp.clip(jax.random.normal(key, (TOKENS, KVH * HD), jnp.float32), -6.0, 6.0)
    return base.astype(jnp.bfloat16)


def draw_page_slot(key, part):
    key = jax.random.fold_in(key, 37)
    total = OWNERS * SLOTS
    inner = 1 + jax.random.permutation(jax.random.fold_in(key, 1), total - 2)[:PAGES - 2]
    chosen = jnp.concatenate([jnp.array([0, total - 1], jnp.int32), inner.astype(jnp.int32)])
    order = jax.random.permutation(jax.random.fold_in(key, 2), PAGES)
    return jnp.take(chosen, order).astype(jnp.int32)


def block_levels(stream_key, extent, pieces, smallest, top_value):
    def one(axis_at, shards_of):
        steps = jax.random.uniform(jax.random.fold_in(jax.random.fold_in(stream_key, 6), axis_at), (shards_of,), jnp.float32, smallest / len(pieces), top_value / len(pieces))
        return jnp.repeat(jnp.exp(steps), extent[axis_at] // shards_of).reshape((-1,) + (1,) * (len(extent) - axis_at - 1))

    factor_of = one(*pieces[0])
    for cut in pieces[1:]:
        factor_of = factor_of * one(*cut)
    return factor_of


def gaussian(rng, shape, deviation, most, cuts=(), kind=jnp.bfloat16):
    values = jax.random.normal(rng, shape, jnp.float32) * deviation
    if len(cuts) > 0:
        values = block_levels(rng, shape, cuts, -0.22, 0.18) * values
    return jnp.clip(values, min=-most, max=most).astype(kind)


def setup_inputs(seed: int = 0) -> dict:
    key_of = jax.random.split(jax.random.key(seed), 5)
    queries = draw_queries(jax.random.fold_in(key_of[4], 71), 0)
    keys = draw_keys(jax.random.fold_in(key_of[4], 71), 0)
    values = gaussian(key_of[2], (TOKENS, KVH * HD), 1.0, 6.0, ((0, 64), (1, 4)))
    page_slot = draw_page_slot(jax.random.fold_in(key_of[4], 71), 0)
    return {"queries": queries, "keys": keys, "values": values, "page_slot": page_slot}


def normalize_pages(rows):
    pages = rows.reshape(PAGES, PAGE, KVH, HD).astype(jnp.float32)
    scale = jnp.max(jnp.abs(pages), axis=(1, 3)) + 1e-6
    normed = (pages / scale[:, None, :, None]).astype(jnp.bfloat16)
    return normed.reshape(PAGES, PAGE * KVH * HD), scale


def place_pages(normed, scale, page_slot):
    cache = jnp.zeros((OWNERS * SLOTS, PAGE * KVH * HD), jnp.bfloat16).at[page_slot].set(normed)
    scales = jnp.zeros((OWNERS * SLOTS, KVH), jnp.float32).at[page_slot].set(scale)
    return cache.reshape(OWNERS * SLOTS * PAGE, KVH * HD), scales


def reference(queries, keys, values, page_slot):
    group = HEADS // KVH
    q_heads = queries.reshape(TOKENS, HEADS, HD)
    k_heads = keys.reshape(TOKENS, KVH, HD)
    v_heads = values.reshape(TOKENS, KVH, HD)
    positions = jnp.arange(TOKENS)
    causal = positions[None, :] <= positions[:, None]

    def one_head(head):
        query = jnp.take(q_heads, head, axis=1)
        key_rows = jnp.take(k_heads, head // group, axis=1)
        value_rows = jnp.take(v_heads, head // group, axis=1)
        scores = jnp.dot(query, key_rows.T, preferred_element_type=jnp.float32) * (HD ** -0.5)
        scores = jnp.where(causal, scores, -1e30)
        rowmax = jnp.max(scores, axis=1, keepdims=True)
        expd = jnp.where(causal, jnp.exp(scores - rowmax), 0.0)
        total = jnp.sum(expd, axis=1, keepdims=True)
        weights = expd.astype(jnp.bfloat16)
        mixed = jnp.dot(weights, value_rows, preferred_element_type=jnp.float32)
        return (mixed / total).astype(jnp.bfloat16)

    outputs = lax.map(one_head, jnp.arange(HEADS).astype(jnp.int32))
    attended = jnp.transpose(outputs, (1, 0, 2)).reshape(TOKENS, HEADS * HD)
    normed_keys, key_scale = normalize_pages(keys)
    normed_values, value_scale = normalize_pages(values)
    cache_keys, key_scales = place_pages(normed_keys, key_scale, page_slot)
    cache_values, value_scales = place_pages(normed_values, value_scale, page_slot)
    return attended, cache_keys, cache_values, key_scales, value_scales
```

```python
import functools

import jax
import jax.numpy as jnp
import numpy as np
from jax import lax
from jax.experimental import pallas as pl
from jax.experimental.pallas import tpu as pltpu
from jax.sharding import PartitionSpec as P

HEADS = 64
KVH = 8
HD = 128
PAGE = 128
TQ = 256
SEG = 512
C = float(np.log2(np.e) / np.sqrt(HD))
NEG = -1e30
LIMIT = 80.0
NT = (((1,), (1,)), ((), ()))


def row_norm(x):
    x = x.astype(jnp.float32)
    return jnp.sqrt(jnp.sum(x * x, axis=1, keepdims=True))


def first_kernel(meta, q_ref, e0, e1, acc_ref, stat_ref):
    rows = q_ref.shape[0]
    core, dec = meta[0], meta[1]
    half = rows // 2
    acc_ref[...] = jnp.zeros_like(acc_ref)
    stat_ref[...] = jnp.zeros_like(stat_ref)
    for h in range(2):
        stat_ref[:, h : h + 1] = jnp.full((rows, 1), NEG, jnp.float32)
        stat_ref[:, 4 + h : 5 + h] = row_norm(q_ref[:, h * HD : (h + 1) * HD])

    def tile(i, _):
        r = pl.ds(pl.multiple_of(i * TQ, TQ), TQ)
        q_pos = i * TQ + lax.broadcasted_iota(jnp.int32, (TQ, 1), 0)
        lane = lax.broadcasted_iota(jnp.int32, (1, SEG), 1)
        ok = []
        for z in range(2):
            page = jnp.bitwise_xor(2 * (lane // PAGE) + z, dec)
            ok.append(core * half + page * PAGE + lane % PAGE <= q_pos)
        allowed = jnp.concatenate(ok, axis=1)
        k = jnp.concatenate([e0[:, :HD], e1[:, :HD]], axis=0)
        v = jnp.concatenate([e0[:, HD:], e1[:, HD:]], axis=0)
        for h in range(2):
            q = q_ref[r, h * HD : (h + 1) * HD]
            s = lax.dot_general(q, k, NT, preferred_element_type=jnp.float32) * C
            s = jnp.where(allowed, s, NEG)
            m = jnp.max(s, axis=1, keepdims=True)
            p = jnp.where(allowed, jnp.exp2(s - m), 0.0)
            acc_ref[r, h * HD : (h + 1) * HD] = jnp.dot(
                p.astype(jnp.bfloat16), v, preferred_element_type=jnp.float32
            )
            stat_ref[r, h : h + 1] = m
            stat_ref[r, 2 + h : 3 + h] = jnp.sum(p, axis=1, keepdims=True)
        return 0

    lax.fori_loop(core * (half // TQ), rows // TQ, tile, 0)


def next_kernel(n, meta, q_ref, *refs):
    segs, acc_in, stat_in, acc_ref, stat_ref = refs[:n], *refs[n:]
    del acc_in, stat_in
    rows = q_ref.shape[0]

    def fast(seg):
        def tile(i, _):
            r = pl.ds(pl.multiple_of(i * TQ, TQ), TQ)
            for h in range(2):
                cols = slice(h * HD, (h + 1) * HD)
                s = lax.dot_general(
                    q_ref[r, cols], seg[:, :HD], NT, preferred_element_type=jnp.float32
                )
                p = jnp.exp2(s * C - stat_ref[r, h : h + 1])
                stat_ref[r, 2 + h : 3 + h] += jnp.sum(p, axis=1, keepdims=True)
                acc_ref[r, cols] += jnp.dot(
                    p.astype(jnp.bfloat16), seg[:, HD:], preferred_element_type=jnp.float32
                )
            return 0

        lax.fori_loop(0, rows // TQ, tile, 0)

    def slow(seg):
        def tile(i, _):
            r = pl.ds(pl.multiple_of(i * TQ, TQ), TQ)
            for h in range(2):
                cols = slice(h * HD, (h + 1) * HD)
                s = C * lax.dot_general(
                    q_ref[r, cols], seg[:, :HD], NT, preferred_element_type=jnp.float32
                )
                old = stat_ref[r, h : h + 1]
                m = jnp.maximum(old, jnp.max(s, axis=1, keepdims=True))
                p = jnp.exp2(s - m)
                a = jnp.exp2(old - m)
                stat_ref[r, h : h + 1] = m
                stat_ref[r, 2 + h : 3 + h] = a * stat_ref[r, 2 + h : 3 + h] + jnp.sum(
                    p, axis=1, keepdims=True
                )
                acc_ref[r, cols] = a * acc_ref[r, cols] + jnp.dot(
                    p.astype(jnp.bfloat16), seg[:, HD:], preferred_element_type=jnp.float32
                )
            return 0

        lax.fori_loop(0, rows // TQ, tile, 0)

    for j, seg in enumerate(segs):

        @pl.when(meta[j] > 0)
        def _():
            longest = jnp.max(row_norm(seg[:, :HD])) * (1.01 * C)
            st = stat_ref[...]
            top = jnp.max(st[:, 4:6] * longest - st[:, 0:2])

            @pl.when(top <= LIMIT)
            def _():
                fast(seg)

            @pl.when(jnp.logical_not(top <= LIMIT))
            def _():
                slow(seg)


def merge_kernel(mine, theirs, ml_mine, ml_theirs, out_ref):
    for h in range(2):
        cols = slice(h * HD, (h + 1) * HD)
        m0, m1 = ml_mine[:, h : h + 1], ml_theirs[:, h : h + 1]
        m = jnp.maximum(m0, m1)
        a0, a1 = jnp.exp2(m0 - m), jnp.exp2(m1 - m)
        total = a0 * ml_mine[:, 2 + h : 3 + h] + a1 * ml_theirs[:, 2 + h : 3 + h]
        mixed = a0 * mine[:, cols] + a1 * theirs[:, cols]
        out_ref[:, cols] = (mixed / total).astype(jnp.bfloat16)


def pick_kernel(meta, *refs):
    pages, outs = refs[:8], refs[8:]
    for d in range(4):
        for j in range(2):
            at = meta[2 * d + j]
            for b in range(8):

                @pl.when(at // 4 == b)
                def _():
                    rows = pl.ds(pl.multiple_of((at % 4) * PAGE, PAGE), PAGE)
                    outs[d][j * PAGE : (j + 1) * PAGE] = pages[b][rows]


def cache_kernel(meta, own, own_c, oth, oth_c, ck, cv, ks, vs):
    col = meta[0]
    scales = [jnp.zeros((2, 2), jnp.float32)] * 2
    row_at = lax.broadcasted_iota(jnp.int32, (2, 2), 0)
    col_at = lax.broadcasted_iota(jnp.int32, (2, 2), 1)
    for j in range(2):
        filled, same = meta[1 + j] > 0, meta[3 + j] > 0
        rows = slice(j * PAGE, (j + 1) * PAGE)
        blocks = [
            jnp.where(same, own[rows], own_c[rows]),
            jnp.where(same, oth[rows], oth_c[rows]),
        ]
        for kind, out in enumerate((ck, cv)):
            normed = []
            for b in range(2):
                x = blocks[b][:, kind * HD : (kind + 1) * HD].astype(jnp.float32)
                x = jnp.where(filled, x, 0.0)
                scale = jnp.max(jnp.abs(x)) + 1e-6
                normed.append((x / scale).astype(jnp.bfloat16))
                here = jnp.logical_and(row_at == j, col_at == (col if b == 0 else 1 - col))
                scales[kind] = jnp.where(jnp.logical_and(here, filled), scale, scales[kind])
            out[rows, :HD] = jnp.where(col == 0, normed[0], normed[1])
            out[rows, HD:] = jnp.where(col == 0, normed[1], normed[0])
    ks[...] = scales[0]
    vs[...] = scales[1]


VMEM = pl.BlockSpec(memory_space=pltpu.VMEM)
SMEM = pl.BlockSpec(memory_space=pltpu.SMEM)
PARAMS = pltpu.CompilerParams(vmem_limit_bytes=48 * 2**20)


def call(kernel, meta, arrays, outs, **more):
    return pl.pallas_call(
        kernel,
        in_specs=[SMEM] + [VMEM] * len(arrays),
        out_specs=[VMEM] * len(outs),
        out_shape=[jax.ShapeDtypeStruct(s, t) for s, t in outs],
        compiler_params=PARAMS,
        **more,
    )(meta, *arrays)


def body(queries, keys, values, page_slot):
    blk, dec = lax.axis_index("blk"), lax.axis_index("dec")
    y, core, head = blk // 2, blk % 2, dec // 4
    tok = queries.shape[0]
    i32 = jnp.int32

    def over_dec(x, m):
        return lax.ppermute(x, "dec", [(i, i ^ m) for i in range(8)])

    def over_core(x):
        return lax.ppermute(x, "blk", [(i, i ^ 1) for i in range(8)])

    def over_y(x, d):
        return lax.ppermute(x, "blk", [(i, (i + 2 * d) % 8) for i in range(8)])

    first = jnp.concatenate([keys[:, :HD], values[:, :HD]], axis=1)
    second = jnp.concatenate([keys[:, HD:], values[:, HD:]], axis=1)
    own = jnp.where(head == 0, first, second)
    other = jnp.where(head == 0, second, first)

    def spread(own, other):
        return jnp.concatenate(
            [own, over_dec(own, 2), over_dec(other, 4), over_dec(other, 6)], axis=0
        )

    across = over_dec(jnp.concatenate([own, other], axis=0), 1)
    e0 = spread(own, other)
    e1 = spread(across[:PAGE], across[PAGE:])
    parts = []
    for e in (e0, e1):
        parts.append((over_y(e, 1), over_y(e, 3), over_y(e, 2)))
    (a0, b0, c0), (a1, b1, c1) = parts

    q_there = over_core(queries)
    q = jnp.where(
        core == 0,
        jnp.concatenate([queries, q_there], axis=0),
        jnp.concatenate([q_there, queries], axis=0),
    )
    state = [((2 * tok, 2 * HD), jnp.float32), ((2 * tok, 8), jnp.float32)]
    acc, stat = call(first_kernel, jnp.stack([core, dec]).astype(i32), [q, e0, e1], state)

    def more(flags, segs, acc, stat):
        n = len(segs)
        return call(
            functools.partial(next_kernel, n),
            jnp.stack(flags).astype(i32),
            [q, *segs, acc, stat],
            state,
            input_output_aliases={n + 2: 0, n + 3: 1},
        )

    below, above, far = y >= 1, y == 3, y >= 2
    acc, stat = more([below, above], [a0, b0], acc, stat)
    acc, stat = more([below, above, far], [a1, b1, c0], acc, stat)
    acc, stat = more([far], [c1], acc, stat)
    lo, hi = slice(0, tok), slice(tok, 2 * tok)
    acc_mine = jnp.where(core == 0, acc[lo], acc[hi])
    acc_theirs = over_core(jnp.where(core == 0, acc[hi], acc[lo]))
    stat_mine = jnp.where(core == 0, stat[lo], stat[hi])
    stat_theirs = over_core(jnp.where(core == 0, stat[hi], stat[lo]))
    attended = pl.pallas_call(
        merge_kernel,
        in_specs=[VMEM] * 4,
        out_specs=VMEM,
        out_shape=jax.ShapeDtypeStruct((tok, 2 * HD), jnp.bfloat16),
        compiler_params=PARAMS,
    )(acc_mine, acc_theirs, stat_mine, stat_theirs)

    owners = jnp.stack(
        [
            8 * (blk ^ dc) + (dec ^ dx)
            for dx in (0, 4)
            for dc in (0, 1)
        ]
    )
    slots = (2 * owners[:, None] + jnp.arange(2)[None, :]).reshape(8)
    hits = page_slot[None, :] == slots[:, None]
    filled = jnp.any(hits, axis=1)
    page = jnp.sum(jnp.where(hits, jnp.arange(64)[None, :], 0), axis=1)
    page_blk, page_dec = page // 8, page % 8
    same = page_blk % 2 == core
    gap = (page_blk // 2 - y) % 4
    rel = page_dec ^ dec
    buffer = 2 * gap + rel % 2
    at = jnp.where(filled & same, 4 * buffer + rel // 2, -1).astype(i32)
    block = ((2 * PAGE, 2 * HD), jnp.bfloat16)
    mine, to_core, to_head, to_both = call(
        pick_kernel, at, [e0, e1, b0, b1, c0, c1, a0, a1], [block] * 4
    )
    own_c = over_core(to_core)
    oth = over_dec(to_head, 4)
    oth_c = lax.ppermute(
        to_both,
        ("blk", "dec"),
        [(8 * b + d, 8 * (b ^ 1) + (d ^ 4)) for b in range(8) for d in range(8)],
    )
    flags = jnp.concatenate([head[None], filled[:2], same[:2]]).astype(i32)
    cache_keys, cache_values, key_scales, value_scales = call(
        cache_kernel,
        flags,
        [mine, own_c, oth, oth_c],
        [block, block, ((2, 2), jnp.float32), ((2, 2), jnp.float32)],
    )
    return attended, cache_keys, cache_values, key_scales, value_scales


def solution(mesh):
    return jax.shard_map(
        body,
        mesh=mesh,
        in_specs=(
            P("blk", ("kvh", "dec")),
            P(("blk", "dec"), "kvh"),
            P(("blk", "dec"), "kvh"),
            P(),
        ),
        out_specs=(
            P("blk", ("kvh", "dec")),
            P(("blk", "dec"), "kvh"),
            P(("blk", "dec"), "kvh"),
            P(("blk", "dec"), "kvh"),
            P(("blk", "dec"), "kvh"),
        ),
        check_vma=False,
    )
```

```python
import functools

import jax
import jax.numpy as jnp
import numpy as np
from jax import lax
from jax.experimental import pallas as pl
from jax.experimental.pallas import tpu as pltpu
from jax.sharding import PartitionSpec as P

HEADS = 64
KVH = 8
HD = 128
PAGE = 128
TQ = 512
TN = 256
TS = 128
SEG = 512
C = float(np.log2(np.e) / np.sqrt(HD))
NEG = -1e30
LIMIT = 80.0
NT = (((1,), (1,)), ((), ()))


def longest(x):
    x = x.astype(jnp.float32)
    squares = jnp.dot(
        (x * x).astype(jnp.bfloat16),
        jnp.ones((HD, HD), jnp.bfloat16),
        preferred_element_type=jnp.float32,
    )
    return jnp.sqrt(jnp.max(squares))


def fast(q_ref, state, h, row, size, k, v, allowed=None):
    acc_ref, shift_ref, total_ref = state[:3]
    q = q_ref[rows_at(row, size), h * HD : (h + 1) * HD]
    r = rows_at(h * q_ref.shape[0] + row, size)
    s = lax.dot_general(q, k, NT, preferred_element_type=jnp.float32)
    p = jnp.exp2(s * C - shift_ref[r])
    if allowed is not None:
        p = jnp.where(allowed, p, 0.0)
    total_ref[r] += jnp.sum(p, axis=1, keepdims=True)
    acc_ref[r] += jnp.dot(p.astype(jnp.bfloat16), v, preferred_element_type=jnp.float32)


def slow(q_ref, state, h, row, size, k, v, allowed=True):
    acc_ref, shift_ref, total_ref = state[:3]
    q = q_ref[rows_at(row, size), h * HD : (h + 1) * HD]
    r = rows_at(h * q_ref.shape[0] + row, size)
    s = C * lax.dot_general(q, k, NT, preferred_element_type=jnp.float32)
    s = jnp.where(allowed, s, NEG)
    total = total_ref[r]
    old = jnp.where(total > 0, shift_ref[r], NEG)
    shift = jnp.maximum(old, jnp.max(s, axis=1, keepdims=True))
    p = jnp.where(allowed, jnp.exp2(s - shift), 0.0)
    a = jnp.exp2(old - shift)
    total = a * total + jnp.sum(p, axis=1, keepdims=True)
    shift_ref[r] = jnp.where(total > 0, shift, 0.0)
    total_ref[r] = total
    acc_ref[r] = a * acc_ref[r] + jnp.dot(
        p.astype(jnp.bfloat16), v, preferred_element_type=jnp.float32
    )


def loop(begin, end, step):
    def one(i, _):
        step(i)
        return 0

    lax.fori_loop(begin, end, one, 0)


def rows_at(start, size):
    return pl.ds(start if isinstance(start, int) else pl.multiple_of(start, size), size)


def guarded(state, key_norm, quick, careful):
    shift_ref, bound_ref = state[1], state[3]
    top = jnp.max(bound_ref[:, 0:1]) * key_norm * (1.02 * C) - jnp.min(bound_ref[:, 1:2])

    @pl.when(top <= LIMIT)
    def _():
        quick()

    @pl.when(jnp.logical_not(top <= LIMIT))
    def _():
        careful()
        lowest = jnp.minimum(jnp.min(shift_ref[...]), 0.0)
        bound_ref[:, 1:2] = jnp.full((8, 1), lowest)


def near_kernel(z, meta, q_ref, e_ref, x_ref, *refs):
    state, page_ref = refs[-5:-1], refs[-1]
    acc_ref, shift_ref, total_ref, bound_ref = state
    rows = q_ref.shape[0]
    core, dec = meta[0], meta[1]
    if z == 0:
        refs[0][...] = q_ref[...]
        acc_ref[...] = jnp.zeros_like(acc_ref)
        shift_ref[...] = jnp.zeros_like(shift_ref)
        total_ref[...] = jnp.zeros_like(total_ref)
        bound_ref[...] = jnp.zeros_like(bound_ref)
        norm = jnp.maximum(longest(q_ref[:, :HD]), longest(q_ref[:, HD:]))
        bound_ref[:, 0:1] = jnp.full((8, 1), norm)
    parity = jnp.bitwise_xor(dec % 2, z)
    for i in range(SEG // PAGE):
        to = jnp.bitwise_xor(dec // 2, i) * PAGE
        page_ref[rows_at(to, PAGE)] = e_ref[i * PAGE : (i + 1) * PAGE]

    def quick():
        row = lax.broadcasted_iota(jnp.int32, (2 * PAGE, PAGE), 0)
        lane = lax.broadcasted_iota(jnp.int32, (2 * PAGE, PAGE), 1)
        last = parity * PAGE + lane <= row
        for t in range(SEG // PAGE):
            n = (t + 1) * PAGE
            allowed = last
            if t:
                allowed = jnp.concatenate([jnp.full((2 * PAGE, t * PAGE), True), last], axis=1)
            for h in range(2):
                fast(
                    q_ref,
                    state,
                    h,
                    t * 2 * PAGE,
                    2 * PAGE,
                    page_ref[:n, :HD],
                    page_ref[:n, HD:],
                    allowed,
                )

        def extra(i):
            for h in range(2):
                fast(q_ref, state, h, i * TQ, TQ, x_ref[:, :HD], x_ref[:, HD:])

        loop(0, jnp.where(core == 1, rows // TQ, 0), extra)

    def careful():
        lane = lax.broadcasted_iota(jnp.int32, (1, SEG), 1)
        key_at = (2 * (lane // PAGE) + parity) * PAGE + lane % PAGE

        def diagonal(i):
            allowed = key_at <= i * TS + lax.broadcasted_iota(jnp.int32, (TS, 1), 0)
            for h in range(2):
                slow(q_ref, state, h, i * TS, TS, page_ref[:, :HD], page_ref[:, HD:], allowed)

        def extra(i):
            for h in range(2):
                slow(q_ref, state, h, i * TS, TS, x_ref[:, :HD], x_ref[:, HD:])

        loop(0, rows // TS, diagonal)
        loop(0, jnp.where(core == 1, rows // TS, 0), extra)

    key_norm = jnp.maximum(longest(e_ref[:, :HD]), longest(x_ref[:, :HD]))
    guarded(state, key_norm, quick, careful)


def next_kernel(last, meta, q_ref, own0, own1, there, *refs):
    if last:
        state, out_ref, kv_ref = refs[-6:-2], *refs[-2:]
    else:
        state, kv_ref = refs[-5:-1], refs[-1]
    rows = q_ref.shape[0]
    count = meta[0]

    for j, own in enumerate((own0, own1)):

        @pl.when(count > j)
        def _():
            kv_ref[2 * j * SEG : (2 * j + 1) * SEG] = own[...]
            kv_ref[(2 * j + 1) * SEG : (2 * j + 2) * SEG] = there[j * SEG : (j + 1) * SEG]

    @pl.when(count > 0)
    def _():
        tiles = rows // TN

        def step(i):
            keys = rows_at((i // tiles) * 2 * SEG, 2 * SEG)
            for h in range(2):
                fast(q_ref, state, h, (i % tiles) * TN, TN, kv_ref[keys, :HD], kv_ref[keys, HD:])

        few = rows // TS

        def slow_step(i):
            keys = rows_at((i // few) * SEG, SEG)
            for h in range(2):
                slow(q_ref, state, h, (i % few) * TS, TS, kv_ref[keys, :HD], kv_ref[keys, HD:])

        norms = [longest(x[:, :HD]) for x in (own0, own1, there)]
        key_norm = jnp.maximum(jnp.maximum(norms[0], norms[1]), norms[2])
        guarded(
            state,
            key_norm,
            lambda: loop(0, count * tiles, step),
            lambda: loop(0, 2 * count * few, slow_step),
        )

    if last:
        acc_ref, _, total_ref, _ = state
        for h in range(2):
            r = slice(h * rows, (h + 1) * rows)
            out_ref[:, h * HD : (h + 1) * HD] = (acc_ref[r] * (1.0 / total_ref[r])).astype(
                jnp.bfloat16
            )


def pick_kernel(meta, *refs):
    pages, outs = refs[:-2], refs[-2:]
    own, (e0, e1, ab0, ab1, cc) = pages[:8], pages[8:]
    places = [(ref, 0) for ref in (*own, e0, e1)]
    places += [(ab0, SEG), (ab1, SEG), (cc, 0), (cc, SEG), (ab0, 0), (ab1, 0)]
    for d in range(2):
        for j in range(2):
            at = meta[2 * d + j]
            for b, (ref, start) in enumerate(places):

                @pl.when(at // 4 == b)
                def _():
                    rows = rows_at(start + (at % 4) * PAGE, PAGE)
                    outs[d][j * PAGE : (j + 1) * PAGE] = ref[rows]


def cache_kernel(meta, own, oth, ck, cv, ks, vs):
    col = meta[0]
    scales = [jnp.zeros((2, 2), jnp.float32)] * 2
    row_at = lax.broadcasted_iota(jnp.int32, (2, 2), 0)
    col_at = lax.broadcasted_iota(jnp.int32, (2, 2), 1)
    for j in range(2):
        filled = meta[1 + j] > 0
        rows = slice(j * PAGE, (j + 1) * PAGE)
        for kind, out in enumerate((ck, cv)):
            normed = []
            for b, block in enumerate((own, oth)):
                x = block[rows, kind * HD : (kind + 1) * HD].astype(jnp.float32)
                x = jnp.where(filled, x, 0.0)
                scale = jnp.max(jnp.abs(x)) + 1e-6
                normed.append((x / scale).astype(jnp.bfloat16))
                here = jnp.logical_and(row_at == j, col_at == (col if b == 0 else 1 - col))
                scales[kind] = jnp.where(jnp.logical_and(here, filled), scale, scales[kind])
            out[rows, :HD] = jnp.where(col == 0, normed[0], normed[1])
            out[rows, HD:] = jnp.where(col == 0, normed[1], normed[0])
    ks[...] = scales[0]
    vs[...] = scales[1]


VMEM = pl.BlockSpec(memory_space=pltpu.VMEM)
SMEM = pl.BlockSpec(memory_space=pltpu.SMEM)
PARAMS = pltpu.CompilerParams(vmem_limit_bytes=10 * 2**20)


def call(kernel, meta, arrays, outs, work=0, **more):
    return pl.pallas_call(
        kernel,
        in_specs=[SMEM] + [VMEM] * len(arrays),
        out_specs=[VMEM] * len(outs),
        out_shape=[jax.ShapeDtypeStruct(s, t) for s, t in outs],
        compiler_params=PARAMS,
        cost_estimate=pl.CostEstimate(flops=4 * HD * work, transcendentals=work, bytes_accessed=2**20),
        **more,
    )(meta, *arrays)


def body(queries, keys, values, page_slot):
    blk, dec = lax.axis_index("blk"), lax.axis_index("dec")
    y, core, head = blk // 2, blk % 2, dec // 4
    tok = queries.shape[0]
    i32 = jnp.int32

    def over_dec(x, m):
        return lax.ppermute(x, "dec", [(i, i ^ m) for i in range(8)])

    def over_core(x):
        return lax.ppermute(x, "blk", [(i, i ^ 1) for i in range(8)])

    def over_y(x, d):
        return lax.ppermute(x, "blk", [(i, (i + 2 * d) % 8) for i in range(8)])

    first = jnp.concatenate([keys[:, :HD], values[:, :HD]], axis=1)
    second = jnp.concatenate([keys[:, HD:], values[:, HD:]], axis=1)
    own = jnp.where(head == 0, first, second)
    other = jnp.where(head == 0, second, first)

    e0 = jnp.concatenate(
        [own, over_dec(own, 2), over_dec(other, 4), over_dec(other, 6)], axis=0
    )

    owners = jnp.stack([8 * blk + dec, 8 * blk + (dec ^ 4)])
    slots = (2 * owners[:, None] + jnp.arange(2)[None, :]).reshape(4)
    hits = page_slot[None, :] == slots[:, None]
    filled = jnp.any(hits, axis=1)
    page = jnp.sum(jnp.where(hits, jnp.arange(64)[None, :], 0), axis=1)
    page_blk, page_dec = page // 8, page % 8
    rel = page_dec ^ dec
    buffer = 8 * ((page_blk % 2) ^ core) + 2 * ((page_blk // 2 - y) % 4) + rel % 2
    at = jnp.where(filled, 4 * buffer + rel // 2, -1).astype(i32)
    flags = jnp.concatenate([head[None], filled[:2]]).astype(i32)

    state_types = [
        ((2 * tok, HD), jnp.float32),
        ((2 * tok, 1), jnp.float32),
        ((2 * tok, 1), jnp.float32),
        ((8, 2), jnp.float32),
    ]
    place = jnp.stack([core, dec]).astype(i32)
    near_by = jnp.where(y == 3, 2, jnp.where(y >= 1, 1, 0)).astype(i32).reshape(1)
    far = jnp.where(y >= 2, 2, 0).astype(i32).reshape(1)
    e0, at, flags, place, near_by, far = lax.optimization_barrier(
        (e0, at, flags, place, near_by, far)
    )
    e0_there = over_core(e0)
    e1 = over_dec(e0, 1)
    e0_y, e0_there = lax.optimization_barrier((e0, e0_there))
    a0, b0 = over_y(e0_y, 1), over_y(e0_y, 3)
    score_count = 2 * tok * SEG

    def near(z, q, e, x, state=()):
        return call(
            functools.partial(near_kernel, z),
            place,
            [q, e, x, *state],
            [((tok, 2 * HD), jnp.bfloat16)] * (z == 0) + state_types,
            2 * score_count,
            scratch_shapes=[pltpu.VMEM((SEG, 2 * HD), jnp.bfloat16)],
            input_output_aliases={4 + i: i for i in range(len(state))},
        )

    def more(count, own0, own1, there, state, last=False):
        return call(
            functools.partial(next_kernel, last),
            count,
            [q, own0, own1, there, *state],
            state_types + [((tok, 2 * HD), jnp.bfloat16)] * last,
            4 * score_count,
            scratch_shapes=[pltpu.VMEM((4 * SEG, 2 * HD), jnp.bfloat16)],
            input_output_aliases={5 + i: i for i in range(4)},
        )

    def both(first, second):
        return over_core(jnp.concatenate([first, second], axis=0))

    q, *state = near(0, queries, e0, e0_there)
    e0_far, state = lax.optimization_barrier((e0, state))
    c0 = over_y(e0_far, 2)
    a0, b0, e1, state = lax.optimization_barrier((a0, b0, e1, state))
    ab0_there = both(a0, b0)
    a1, b1 = over_y(e1, 1), over_y(e1, 3)
    e1_there = over_core(e1)
    state = more(near_by, a0, b0, ab0_there, state)
    e1_far, state = lax.optimization_barrier((e1, state))
    c1 = over_y(e1_far, 2)
    a1, b1, state = lax.optimization_barrier((a1, b1, state))
    ab1_there = both(a1, b1)
    state = near(1, q, e1, e1_there, state)
    state = more(near_by, a1, b1, ab1_there, state)
    c0, c1, state = lax.optimization_barrier((c0, c1, state))
    c_there = both(c0, c1)

    block = ((2 * PAGE, 2 * HD), jnp.bfloat16)
    at, state = lax.optimization_barrier((at, state))
    mine, to_head = call(
        pick_kernel,
        at,
        [e0, e1, b0, b1, c0, c1, a0, a1, e0_there, e1_there, ab0_there, ab1_there, c_there],
        [block] * 2,
    )
    state, mine = lax.optimization_barrier((state, mine))
    oth = over_dec(to_head, 4)
    *_, attended = more(far, c0, c1, c_there, state, True)
    cache_keys, cache_values, key_scales, value_scales = call(
        cache_kernel,
        flags,
        [mine, oth],
        [block, block, ((2, 2), jnp.float32), ((2, 2), jnp.float32)],
    )
    return attended, cache_keys, cache_values, key_scales, value_scales


def solution(mesh):
    return jax.shard_map(
        body,
        mesh=mesh,
        in_specs=(
            P("blk", ("kvh", "dec")),
            P(("blk", "dec"), "kvh"),
            P(("blk", "dec"), "kvh"),
            P(),
        ),
        out_specs=(
            P("blk", ("kvh", "dec")),
            P(("blk", "dec"), "kvh"),
            P(("blk", "dec"), "kvh"),
            P(("blk", "dec"), "kvh"),
            P(("blk", "dec"), "kvh"),
        ),
        check_vma=False,
    )
```

```python
import functools

import jax
import jax.numpy as jnp
import numpy as np
from jax import lax
from jax.experimental import pallas as pl
from jax.experimental.pallas import tpu as pltpu
from jax.sharding import PartitionSpec as P

HEADS = 64
KVH = 8
HD = 128
PAGE = 128
TQ = 512
TN = 256
TS = 128
SEG = 512
C = float(np.log2(np.e) / np.sqrt(HD))
NEG = -1e30
LIMIT = 80.0
NT = (((1,), (1,)), ((), ()))


def longest(x):
    x = x.astype(jnp.float32)
    squares = jnp.dot(
        (x * x).astype(jnp.bfloat16),
        jnp.ones((HD, HD), jnp.bfloat16),
        preferred_element_type=jnp.float32,
    )
    return jnp.sqrt(jnp.max(squares))


def fast(q_ref, state, h, row, size, k, v, allowed=None):
    acc_ref, shift_ref, total_ref = state[:3]
    q = q_ref[rows_at(row, size), h * HD : (h + 1) * HD]
    r = rows_at(h * q_ref.shape[0] + row, size)
    s = lax.dot_general(q, k, NT, preferred_element_type=jnp.float32)
    p = jnp.exp2(s * C - shift_ref[r])
    if allowed is not None:
        p = jnp.where(allowed, p, 0.0)
    total_ref[r] += jnp.sum(p, axis=1, keepdims=True)
    acc_ref[r] += jnp.dot(p.astype(jnp.bfloat16), v, preferred_element_type=jnp.float32)


def slow(q_ref, state, h, row, size, k, v, allowed=True):
    acc_ref, shift_ref, total_ref = state[:3]
    q = q_ref[rows_at(row, size), h * HD : (h + 1) * HD]
    r = rows_at(h * q_ref.shape[0] + row, size)
    s = C * lax.dot_general(q, k, NT, preferred_element_type=jnp.float32)
    s = jnp.where(allowed, s, NEG)
    total = total_ref[r]
    old = jnp.where(total > 0, shift_ref[r], NEG)
    shift = jnp.maximum(old, jnp.max(s, axis=1, keepdims=True))
    p = jnp.where(allowed, jnp.exp2(s - shift), 0.0)
    a = jnp.exp2(old - shift)
    total = a * total + jnp.sum(p, axis=1, keepdims=True)
    shift_ref[r] = jnp.where(total > 0, shift, 0.0)
    total_ref[r] = total
    acc_ref[r] = a * acc_ref[r] + jnp.dot(
        p.astype(jnp.bfloat16), v, preferred_element_type=jnp.float32
    )


def loop(begin, end, step):
    def one(i, _):
        step(i)
        return 0

    lax.fori_loop(begin, end, one, 0)


def rows_at(start, size):
    return pl.ds(start if isinstance(start, int) else pl.multiple_of(start, size), size)


def guarded(state, key_norm, quick, careful):
    shift_ref, bound_ref = state[1], state[3]
    top = jnp.max(bound_ref[:, 0:1]) * key_norm * (1.02 * C) - jnp.min(bound_ref[:, 1:2])

    @pl.when(top <= LIMIT)
    def _():
        quick()

    @pl.when(jnp.logical_not(top <= LIMIT))
    def _():
        careful()
        lowest = jnp.minimum(jnp.min(shift_ref[...]), 0.0)
        bound_ref[:, 1:2] = jnp.full((8, 1), lowest)


def fill(meta, arrays, kv_ref, units):
    for u, unit in enumerate(units):
        for j, choices in enumerate(unit):
            for use, (i, row) in enumerate(choices):
                wanted = meta[0] > u
                if len(choices) > 1:
                    wanted = jnp.logical_and(wanted, meta[1] == use)

                @pl.when(wanted)
                def _():
                    at = (2 * u + j) * SEG
                    kv_ref[at : at + SEG] = arrays[i][row : row + SEG]


def norm_of(kv_ref, count):
    norms = [longest(kv_ref[at : at + 2 * SEG, :HD]) for at in range(0, kv_ref.shape[0], 2 * SEG)]
    norm = jnp.where(count > 0, norms[0], 0.0)
    for u in range(1, len(norms)):
        norm = jnp.maximum(norm, jnp.where(count > u, norms[u], 0.0))
    return norm


def units_quick(q_ref, state, kv_ref, count):
    tiles = q_ref.shape[0] // TN

    def step(i):
        keys = rows_at((i // tiles) * 2 * SEG, 2 * SEG)
        for h in range(2):
            fast(q_ref, state, h, (i % tiles) * TN, TN, kv_ref[keys, :HD], kv_ref[keys, HD:])

    loop(0, count * tiles, step)


def units_careful(q_ref, state, kv_ref, count):
    few = q_ref.shape[0] // TS

    def step(i):
        keys = rows_at((i // few) * SEG, SEG)
        for h in range(2):
            slow(q_ref, state, h, (i % few) * TS, TS, kv_ref[keys, :HD], kv_ref[keys, HD:])

    loop(0, 2 * count * few, step)


def near_kernel(z, units, meta, q_ref, e_ref, x_ref, *refs):
    count = 0
    if units:
        kv_ref, arrays = refs[-1], refs[: len(refs) - 10]
        refs = refs[:-1]
        count = meta[0]
        fill(meta, arrays, kv_ref, units)
    state, page_ref = refs[-5:-1], refs[-1]
    acc_ref, shift_ref, total_ref, bound_ref = state
    rows = q_ref.shape[0]
    core, dec = meta[2], meta[3]
    if z == 0:
        refs[0][...] = q_ref[...]
        acc_ref[...] = jnp.zeros_like(acc_ref)
        shift_ref[...] = jnp.zeros_like(shift_ref)
        total_ref[...] = jnp.zeros_like(total_ref)
        bound_ref[...] = jnp.zeros_like(bound_ref)
        norm = jnp.maximum(longest(q_ref[:, :HD]), longest(q_ref[:, HD:]))
        bound_ref[:, 0:1] = jnp.full((8, 1), norm)
    parity = jnp.bitwise_xor(dec % 2, z)
    for i in range(SEG // PAGE):
        to = jnp.bitwise_xor(dec // 2, i) * PAGE
        page_ref[rows_at(to, PAGE)] = e_ref[i * PAGE : (i + 1) * PAGE]

    def quick():
        row = lax.broadcasted_iota(jnp.int32, (2 * PAGE, PAGE), 0)
        lane = lax.broadcasted_iota(jnp.int32, (2 * PAGE, PAGE), 1)
        last = parity * PAGE + lane <= row
        for t in range(SEG // PAGE):
            n = (t + 1) * PAGE
            allowed = last
            if t:
                allowed = jnp.concatenate([jnp.full((2 * PAGE, t * PAGE), True), last], axis=1)
            for h in range(2):
                fast(
                    q_ref,
                    state,
                    h,
                    t * 2 * PAGE,
                    2 * PAGE,
                    page_ref[:n, :HD],
                    page_ref[:n, HD:],
                    allowed,
                )

        def extra(i):
            for h in range(2):
                fast(q_ref, state, h, i * TQ, TQ, x_ref[:, :HD], x_ref[:, HD:])

        loop(0, jnp.where(core == 1, rows // TQ, 0), extra)
        if units:
            units_quick(q_ref, state, kv_ref, count)

    def careful():
        lane = lax.broadcasted_iota(jnp.int32, (1, SEG), 1)
        key_at = (2 * (lane // PAGE) + parity) * PAGE + lane % PAGE

        def diagonal(i):
            allowed = key_at <= i * TS + lax.broadcasted_iota(jnp.int32, (TS, 1), 0)
            for h in range(2):
                slow(q_ref, state, h, i * TS, TS, page_ref[:, :HD], page_ref[:, HD:], allowed)

        def extra(i):
            for h in range(2):
                slow(q_ref, state, h, i * TS, TS, x_ref[:, :HD], x_ref[:, HD:])

        loop(0, rows // TS, diagonal)
        loop(0, jnp.where(core == 1, rows // TS, 0), extra)
        if units:
            units_careful(q_ref, state, kv_ref, count)

    key_norm = jnp.maximum(longest(e_ref[:, :HD]), longest(x_ref[:, :HD]))
    if units:
        key_norm = jnp.maximum(key_norm, norm_of(kv_ref, count))
    guarded(state, key_norm, quick, careful)


def next_kernel(n, units, last, meta, q_ref, *refs):
    arrays = refs[:n]
    if last:
        state, out_ref, kv_ref = refs[-6:-2], *refs[-2:]
    else:
        state, kv_ref = refs[-5:-1], refs[-1]
    rows = q_ref.shape[0]
    count = meta[0]

    @pl.when(count > 0)
    def _():
        fill(meta, arrays, kv_ref, units)
        guarded(
            state,
            norm_of(kv_ref, count),
            lambda: units_quick(q_ref, state, kv_ref, count),
            lambda: units_careful(q_ref, state, kv_ref, count),
        )

    if last:
        acc_ref, _, total_ref, _ = state
        for h in range(2):
            r = slice(h * rows, (h + 1) * rows)
            out_ref[:, h * HD : (h + 1) * HD] = (acc_ref[r] * (1.0 / total_ref[r])).astype(
                jnp.bfloat16
            )


def pick_kernel(meta, *refs):
    pages, outs = refs[:-2], refs[-2:]
    own, (e0, e1, c0, c1, ab0, ab1) = pages[:8], pages[8:]
    places = [(ref, 0) for ref in (*own, e0, e1)]
    places += [(ab0, SEG), (ab1, SEG), (c0, 0), (c1, 0), (ab0, 0), (ab1, 0)]
    for d in range(2):
        for j in range(2):
            at = meta[2 * d + j]
            for b, (ref, start) in enumerate(places):

                @pl.when(at // 4 == b)
                def _():
                    rows = rows_at(start + (at % 4) * PAGE, PAGE)
                    outs[d][j * PAGE : (j + 1) * PAGE] = ref[rows]


def cache_kernel(meta, own, oth, ck, cv, ks, vs):
    col = meta[0]
    scales = [jnp.zeros((2, 2), jnp.float32)] * 2
    row_at = lax.broadcasted_iota(jnp.int32, (2, 2), 0)
    col_at = lax.broadcasted_iota(jnp.int32, (2, 2), 1)
    for j in range(2):
        filled = meta[1 + j] > 0
        rows = slice(j * PAGE, (j + 1) * PAGE)
        for kind, out in enumerate((ck, cv)):
            normed = []
            for b, block in enumerate((own, oth)):
                x = block[rows, kind * HD : (kind + 1) * HD].astype(jnp.float32)
                x = jnp.where(filled, x, 0.0)
                scale = jnp.max(jnp.abs(x)) + 1e-6
                normed.append((x / scale).astype(jnp.bfloat16))
                here = jnp.logical_and(row_at == j, col_at == (col if b == 0 else 1 - col))
                scales[kind] = jnp.where(jnp.logical_and(here, filled), scale, scales[kind])
            out[rows, :HD] = jnp.where(col == 0, normed[0], normed[1])
            out[rows, HD:] = jnp.where(col == 0, normed[1], normed[0])
    ks[...] = scales[0]
    vs[...] = scales[1]


VMEM = pl.BlockSpec(memory_space=pltpu.VMEM)
SMEM = pl.BlockSpec(memory_space=pltpu.SMEM)
PARAMS = pltpu.CompilerParams(vmem_limit_bytes=10 * 2**20)


def call(kernel, meta, arrays, outs, **more):
    return pl.pallas_call(
        kernel,
        in_specs=[SMEM] + [VMEM] * len(arrays),
        out_specs=[VMEM] * len(outs),
        out_shape=[jax.ShapeDtypeStruct(s, t) for s, t in outs],
        compiler_params=PARAMS,
        **more,
    )(meta, *arrays)


def body(queries, keys, values, page_slot):
    blk, dec = lax.axis_index("blk"), lax.axis_index("dec")
    y, core, head = blk // 2, blk % 2, dec // 4
    tok = queries.shape[0]
    i32 = jnp.int32

    def over_dec(x, m):
        return lax.ppermute(x, "dec", [(i, i ^ m) for i in range(8)])

    def over_core(x):
        return lax.ppermute(x, "blk", [(i, i ^ 1) for i in range(8)])

    def over_y(x, d):
        return lax.ppermute(x, "blk", [(i, (i + 2 * d) % 8) for i in range(8)])

    first = jnp.concatenate([keys[:, :HD], values[:, :HD]], axis=1)
    second = jnp.concatenate([keys[:, HD:], values[:, HD:]], axis=1)
    own = jnp.where(head == 0, first, second)
    other = jnp.where(head == 0, second, first)

    e0 = jnp.concatenate(
        [own, over_dec(own, 2), over_dec(other, 4), over_dec(other, 6)], axis=0
    )

    owners = jnp.stack([8 * blk + dec, 8 * blk + (dec ^ 4)])
    slots = (2 * owners[:, None] + jnp.arange(2)[None, :]).reshape(4)
    hits = page_slot[None, :] == slots[:, None]
    filled = jnp.any(hits, axis=1)
    page = jnp.sum(jnp.where(hits, jnp.arange(64)[None, :], 0), axis=1)
    page_blk, page_dec = page // 8, page % 8
    rel = page_dec ^ dec
    buffer = 8 * ((page_blk % 2) ^ core) + 2 * ((page_blk // 2 - y) % 4) + rel % 2
    at = jnp.where(filled, 4 * buffer + rel // 2, -1).astype(i32)
    flags = jnp.concatenate([head[None], filled[:2]]).astype(i32)

    state_types = [
        ((2 * tok, HD), jnp.float32),
        ((2 * tok, 1), jnp.float32),
        ((2 * tok, 1), jnp.float32),
        ((8, 2), jnp.float32),
    ]
    def meta_of(count, other):
        return jnp.stack([count + 0 * y, other + 0 * y, core, dec]).astype(i32)

    top = jnp.where(y == 3, 1, 0)
    some = jnp.where(y >= 1, 1, 0)
    place = meta_of(0, 0)
    above = meta_of(top, top)
    below = meta_of(some, top)
    below_above = meta_of(some + top, top)
    far = meta_of(jnp.where(y >= 2, 1, 0), 0)
    e0, at, flags, place, above, below, below_above, far = lax.optimization_barrier(
        (e0, at, flags, place, above, below, below_above, far)
    )
    e0_there = over_core(e0)
    e1 = over_dec(e0, 1)
    a0, b0 = over_y(e0, 1), over_y(e0, 3)
    e0_far, e0_there = lax.optimization_barrier((e0, e0_there))
    c0 = over_y(e0_far, 2)

    def near(z, meta, q, e, x, arrays=(), units=(), state=()):
        n = len(arrays)
        kv = [pltpu.VMEM((2 * len(units) * SEG, 2 * HD), jnp.bfloat16)] if units else []
        return call(
            functools.partial(near_kernel, z, units),
            meta,
            [q, e, x, *arrays, *state],
            [((tok, 2 * HD), jnp.bfloat16)] * (z == 0) + state_types,
            scratch_shapes=[pltpu.VMEM((SEG, 2 * HD), jnp.bfloat16), *kv],
            input_output_aliases={n + 4 + i: i for i in range(len(state))},
        )

    def more(meta, arrays, units, state, last=False):
        n = len(arrays)
        return call(
            functools.partial(next_kernel, n, units, last),
            meta,
            [q, *arrays, *state],
            state_types + [((tok, 2 * HD), jnp.bfloat16)] * last,
            scratch_shapes=[pltpu.VMEM((2 * len(units) * SEG, 2 * HD), jnp.bfloat16)],
            input_output_aliases={n + 2 + i: i for i in range(4)},
        )

    def both(first, second):
        return over_core(jnp.concatenate([first, second], axis=0))

    pair = [((0, 0),), ((1, 0),)]
    crossed = [((0, 0), (2, SEG)), ((2, 0),)]
    q, *state = near(0, place, queries, e0, e0_there)
    state = more(above, [a0, b0], [pair], state)
    a0, b0, c0, e1, state = lax.optimization_barrier((a0, b0, c0, e1, state))
    ab0_there = both(a0, b0)
    a1, b1 = over_y(e1, 1), over_y(e1, 3)
    e1_there, c0_there = over_core(e1), over_core(c0)
    e1_there, c0_there, state = lax.optimization_barrier((e1_there, c0_there, state))
    state = near(1, below, q, e1, e1_there, [a0, b0, ab0_there], [crossed], state)
    a1, b1, state = lax.optimization_barrier((a1, b1, state))
    ab1_there = both(a1, b1)
    e1_far, a1 = lax.optimization_barrier((e1, a1))
    c1 = over_y(e1_far, 2)
    state = more(far, [c0, c0_there], [pair], state)
    state = more(below_above, [a1, b1, ab1_there], [crossed, pair], state)
    c1, state = lax.optimization_barrier((c1, state))
    c1_there = over_core(c1)

    block = ((2 * PAGE, 2 * HD), jnp.bfloat16)
    at, state = lax.optimization_barrier((at, state))
    mine, to_head = call(
        pick_kernel,
        at,
        [e0, e1, b0, b1, c0, c1, a0, a1, e0_there, e1_there, c0_there, c1_there, ab0_there, ab1_there],
        [block] * 2,
    )
    state, mine = lax.optimization_barrier((state, mine))
    oth = over_dec(to_head, 4)
    *_, attended = more(far, [c1, c1_there], [pair], state, True)
    cache_keys, cache_values, key_scales, value_scales = call(
        cache_kernel,
        flags,
        [mine, oth],
        [block, block, ((2, 2), jnp.float32), ((2, 2), jnp.float32)],
    )
    return attended, cache_keys, cache_values, key_scales, value_scales


def solution(mesh):
    return jax.shard_map(
        body,
        mesh=mesh,
        in_specs=(
            P("blk", ("kvh", "dec")),
            P(("blk", "dec"), "kvh"),
            P(("blk", "dec"), "kvh"),
            P(),
        ),
        out_specs=(
            P("blk", ("kvh", "dec")),
            P(("blk", "dec"), "kvh"),
            P(("blk", "dec"), "kvh"),
            P(("blk", "dec"), "kvh"),
            P(("blk", "dec"), "kvh"),
        ),
        check_vma=False,
    )
```

```python
import functools

import jax
import jax.numpy as jnp
import numpy as np
from jax import lax
from jax.experimental import pallas as pl
from jax.experimental.pallas import tpu as pltpu
from jax.sharding import PartitionSpec as P

HEADS = 64
KVH = 8
HD = 128
PAGE = 128
TQ = 512
TN = 256
TS = 128
SEG = 512
C = float(np.log2(np.e) / np.sqrt(HD))
NEG = -1e30
LIMIT = 80.0
NT = (((1,), (1,)), ((), ()))


def longest(x):
    x = x.astype(jnp.float32)
    squares = jnp.dot(
        (x * x).astype(jnp.bfloat16),
        jnp.ones((HD, HD), jnp.bfloat16),
        preferred_element_type=jnp.float32,
    )
    return jnp.sqrt(jnp.max(squares))


def fast(q_ref, state, h, row, size, k, v, allowed=None):
    acc_ref, shift_ref, total_ref = state[:3]
    q = q_ref[rows_at(row, size), h * HD : (h + 1) * HD]
    r = rows_at(h * q_ref.shape[0] + row, size)
    s = lax.dot_general(q, k, NT, preferred_element_type=jnp.float32)
    p = jnp.exp2(s * C - shift_ref[r])
    if allowed is not None:
        p = jnp.where(allowed, p, 0.0)
    total_ref[r] += jnp.sum(p, axis=1, keepdims=True)
    acc_ref[r] += jnp.dot(p.astype(jnp.bfloat16), v, preferred_element_type=jnp.float32)


def slow(q_ref, state, h, row, size, k, v, allowed=True):
    acc_ref, shift_ref, total_ref = state[:3]
    q = q_ref[rows_at(row, size), h * HD : (h + 1) * HD]
    r = rows_at(h * q_ref.shape[0] + row, size)
    s = C * lax.dot_general(q, k, NT, preferred_element_type=jnp.float32)
    s = jnp.where(allowed, s, NEG)
    total = total_ref[r]
    old = jnp.where(total > 0, shift_ref[r], NEG)
    shift = jnp.maximum(old, jnp.max(s, axis=1, keepdims=True))
    p = jnp.where(allowed, jnp.exp2(s - shift), 0.0)
    a = jnp.exp2(old - shift)
    total = a * total + jnp.sum(p, axis=1, keepdims=True)
    shift_ref[r] = jnp.where(total > 0, shift, 0.0)
    total_ref[r] = total
    acc_ref[r] = a * acc_ref[r] + jnp.dot(
        p.astype(jnp.bfloat16), v, preferred_element_type=jnp.float32
    )


def loop(begin, end, step):
    def one(i, _):
        step(i)
        return 0

    lax.fori_loop(begin, end, one, 0)


def rows_at(start, size):
    return pl.ds(start if isinstance(start, int) else pl.multiple_of(start, size), size)


def guarded(state, key_norm, quick, careful):
    shift_ref, bound_ref = state[1], state[3]
    top = jnp.max(bound_ref[:, 0:1]) * key_norm * (1.02 * C) - jnp.min(bound_ref[:, 1:2])

    @pl.when(top <= LIMIT)
    def _():
        quick()

    @pl.when(jnp.logical_not(top <= LIMIT))
    def _():
        careful()
        lowest = jnp.minimum(jnp.min(shift_ref[...]), 0.0)
        bound_ref[:, 1:2] = jnp.full((8, 1), lowest)


def fill(meta, arrays, kv_ref, units):
    for u, unit in enumerate(units):
        for j, choices in enumerate(unit):
            for use, (i, row) in enumerate(choices):
                wanted = meta[0] > u
                if len(choices) > 1:
                    wanted = jnp.logical_and(wanted, meta[1] == use)

                @pl.when(wanted)
                def _():
                    at = (2 * u + j) * SEG
                    kv_ref[at : at + SEG] = arrays[i][row : row + SEG]


def norm_of(kv_ref, count):
    norms = [longest(kv_ref[at : at + 2 * SEG, :HD]) for at in range(0, kv_ref.shape[0], 2 * SEG)]
    norm = jnp.where(count > 0, norms[0], 0.0)
    for u in range(1, len(norms)):
        norm = jnp.maximum(norm, jnp.where(count > u, norms[u], 0.0))
    return norm


def units_quick(q_ref, state, kv_ref, count, finish=None):
    tiles = q_ref.shape[0] // (2 * TN)

    def step(i):
        keys = rows_at((i // tiles) * 2 * SEG, 2 * SEG)
        for part in range(2):
            row = (i % tiles) * 2 * TN + part * TN
            for h in range(2):
                fast(q_ref, state, h, row, TN, kv_ref[keys, :HD], kv_ref[keys, HD:])
                if finish is not None:
                    finish(h, row, TN)

    loop(0, count * tiles, step)


def units_careful(q_ref, state, kv_ref, count):
    few = q_ref.shape[0] // TS

    def step(i):
        keys = rows_at((i // few) * SEG, SEG)
        for h in range(2):
            slow(q_ref, state, h, (i % few) * TS, TS, kv_ref[keys, :HD], kv_ref[keys, HD:])

    loop(0, 2 * count * few, step)


def near_kernel(z, units, meta, q_ref, e_ref, x_ref, *refs):
    count = 0
    if units:
        kv_ref, arrays = refs[-1], refs[: len(refs) - 10]
        refs = refs[:-1]
        count = meta[0]
        fill(meta, arrays, kv_ref, units)
    state, page_ref = refs[-5:-1], refs[-1]
    acc_ref, shift_ref, total_ref, bound_ref = state
    rows = q_ref.shape[0]
    core, dec = meta[2], meta[3]
    if z == 0:
        refs[0][...] = q_ref[...]
        acc_ref[...] = jnp.zeros_like(acc_ref)
        shift_ref[...] = jnp.zeros_like(shift_ref)
        total_ref[...] = jnp.zeros_like(total_ref)
        bound_ref[...] = jnp.zeros_like(bound_ref)
        norm = jnp.maximum(longest(q_ref[:, :HD]), longest(q_ref[:, HD:]))
        bound_ref[:, 0:1] = jnp.full((8, 1), norm)
    parity = jnp.bitwise_xor(dec % 2, z)
    for i in range(SEG // PAGE):
        to = jnp.bitwise_xor(dec // 2, i) * PAGE
        page_ref[rows_at(to, PAGE)] = e_ref[i * PAGE : (i + 1) * PAGE]

    def quick():
        row = lax.broadcasted_iota(jnp.int32, (2 * PAGE, PAGE), 0)
        lane = lax.broadcasted_iota(jnp.int32, (2 * PAGE, PAGE), 1)
        last = parity * PAGE + lane <= row
        for t in range(SEG // PAGE):
            n = (t + 1) * PAGE
            allowed = last
            if t:
                allowed = jnp.concatenate([jnp.full((2 * PAGE, t * PAGE), True), last], axis=1)
            for h in range(2):
                fast(
                    q_ref,
                    state,
                    h,
                    t * 2 * PAGE,
                    2 * PAGE,
                    page_ref[:n, :HD],
                    page_ref[:n, HD:],
                    allowed,
                )

        def extra(i):
            for h in range(2):
                fast(q_ref, state, h, i * TQ, TQ, x_ref[:, :HD], x_ref[:, HD:])

        loop(0, jnp.where(core == 1, rows // TQ, 0), extra)
        if units:
            units_quick(q_ref, state, kv_ref, count)

    def careful():
        lane = lax.broadcasted_iota(jnp.int32, (1, SEG), 1)
        key_at = (2 * (lane // PAGE) + parity) * PAGE + lane % PAGE

        def diagonal(i):
            allowed = key_at <= i * TS + lax.broadcasted_iota(jnp.int32, (TS, 1), 0)
            for h in range(2):
                slow(q_ref, state, h, i * TS, TS, page_ref[:, :HD], page_ref[:, HD:], allowed)

        def extra(i):
            for h in range(2):
                slow(q_ref, state, h, i * TS, TS, x_ref[:, :HD], x_ref[:, HD:])

        loop(0, rows // TS, diagonal)
        loop(0, jnp.where(core == 1, rows // TS, 0), extra)
        if units:
            units_careful(q_ref, state, kv_ref, count)

    key_norm = jnp.maximum(longest(e_ref[:, :HD]), longest(x_ref[:, :HD]))
    if units:
        key_norm = jnp.maximum(key_norm, norm_of(kv_ref, count))
    guarded(state, key_norm, quick, careful)


def next_kernel(n, units, last, meta, q_ref, *refs):
    arrays = refs[:n]
    if last:
        state, out_ref, kv_ref = refs[-6:-2], *refs[-2:]
    else:
        state, kv_ref = refs[-5:-1], refs[-1]
    rows = q_ref.shape[0]
    count = meta[0]

    def finish(h, row, size):
        r = rows_at(h * rows + row, size)
        mean = state[0][r] * (1.0 / state[2][r])
        out_ref[rows_at(row, size), h * HD : (h + 1) * HD] = mean.astype(jnp.bfloat16)

    def finish_all():
        def step(i):
            for h in range(2):
                finish(h, i * TN, TN)

        loop(0, rows // TN, step)

    def careful():
        units_careful(q_ref, state, kv_ref, count)
        if last:
            finish_all()

    @pl.when(count > 0)
    def _():
        fill(meta, arrays, kv_ref, units)
        guarded(
            state,
            norm_of(kv_ref, count),
            lambda: units_quick(q_ref, state, kv_ref, count, finish if last else None),
            careful,
        )

    if last:
        pl.when(count == 0)(finish_all)


def pick_kernel(meta, *refs):
    pages, outs = refs[:-2], refs[-2:]
    own, (e0, e1, c0, c1, ab0, ab1) = pages[:8], pages[8:]
    places = [(ref, 0) for ref in (*own, e0, e1)]
    places += [(ab0, SEG), (ab1, SEG), (c0, 0), (c1, 0), (ab0, 0), (ab1, 0)]
    for d in range(2):
        for j in range(2):
            at = meta[2 * d + j]
            for b, (ref, start) in enumerate(places):

                @pl.when(at // 4 == b)
                def _():
                    rows = rows_at(start + (at % 4) * PAGE, PAGE)
                    outs[d][j * PAGE : (j + 1) * PAGE] = ref[rows]


def cache_kernel(meta, own, oth, ck, cv, ks, vs):
    col = meta[0]
    scales = [jnp.zeros((2, 2), jnp.float32)] * 2
    row_at = lax.broadcasted_iota(jnp.int32, (2, 2), 0)
    col_at = lax.broadcasted_iota(jnp.int32, (2, 2), 1)
    for j in range(2):
        filled = meta[1 + j] > 0
        rows = slice(j * PAGE, (j + 1) * PAGE)
        for kind, out in enumerate((ck, cv)):
            normed = []
            for b, block in enumerate((own, oth)):
                x = block[rows, kind * HD : (kind + 1) * HD].astype(jnp.float32)
                x = jnp.where(filled, x, 0.0)
                scale = jnp.max(jnp.abs(x), keepdims=True) + 1e-6
                normed.append((x / scale).astype(jnp.bfloat16))
                here = jnp.logical_and(row_at == j, col_at == (col if b == 0 else 1 - col))
                scales[kind] = jnp.where(jnp.logical_and(here, filled), scale, scales[kind])
            out[rows, :HD] = jnp.where(col == 0, normed[0], normed[1])
            out[rows, HD:] = jnp.where(col == 0, normed[1], normed[0])
    ks[...] = scales[0]
    vs[...] = scales[1]


VMEM = pl.BlockSpec(memory_space=pltpu.VMEM)
SMEM = pl.BlockSpec(memory_space=pltpu.SMEM)
PARAMS = pltpu.CompilerParams(vmem_limit_bytes=10 * 2**20)


def call(kernel, meta, arrays, outs, **more):
    return pl.pallas_call(
        kernel,
        in_specs=[SMEM] + [VMEM] * len(arrays),
        out_specs=[VMEM] * len(outs),
        out_shape=[jax.ShapeDtypeStruct(s, t) for s, t in outs],
        compiler_params=PARAMS,
        **more,
    )(meta, *arrays)


def body(queries, keys, values, page_slot):
    blk, dec = lax.axis_index("blk"), lax.axis_index("dec")
    y, core, head = blk // 2, blk % 2, dec // 4
    tok = queries.shape[0]
    i32 = jnp.int32

    def over_dec(x, m):
        return lax.ppermute(x, "dec", [(i, i ^ m) for i in range(8)])

    def over_core(x):
        return lax.ppermute(x, "blk", [(i, i ^ 1) for i in range(8)])

    def over_y(x, d):
        return lax.ppermute(x, "blk", [(i, (i + 2 * d) % 8) for i in range(8)])

    first = jnp.concatenate([keys[:, :HD], values[:, :HD]], axis=1)
    second = jnp.concatenate([keys[:, HD:], values[:, HD:]], axis=1)
    own = jnp.where(head == 0, first, second)
    other = jnp.where(head == 0, second, first)

    e0 = jnp.concatenate(
        [own, over_dec(own, 2), over_dec(other, 4), over_dec(other, 6)], axis=0
    )

    owners = jnp.stack([8 * blk + dec, 8 * blk + (dec ^ 4)])
    slots = (2 * owners[:, None] + jnp.arange(2)[None, :]).reshape(4)
    hits = page_slot[None, :] == slots[:, None]
    filled = jnp.any(hits, axis=1)
    page = jnp.sum(jnp.where(hits, jnp.arange(64)[None, :], 0), axis=1)
    page_blk, page_dec = page // 8, page % 8
    rel = page_dec ^ dec
    buffer = 8 * ((page_blk % 2) ^ core) + 2 * ((page_blk // 2 - y) % 4) + rel % 2
    at = jnp.where(filled, 4 * buffer + rel // 2, -1).astype(i32)
    flags = jnp.concatenate([head[None], filled[:2]]).astype(i32)

    state_types = [
        ((2 * tok, HD), jnp.float32),
        ((2 * tok, 1), jnp.float32),
        ((2 * tok, 1), jnp.float32),
        ((8, 2), jnp.float32),
    ]
    def meta_of(count, other):
        return jnp.stack([count + 0 * y, other + 0 * y, core, dec]).astype(i32)

    top = jnp.where(y == 3, 1, 0)
    some = jnp.where(y >= 1, 1, 0)
    place = meta_of(0, 0)
    above = meta_of(top, top)
    below_above = meta_of(some + top, top)
    below_far = meta_of(some + jnp.where(y >= 2, 1, 0), top)
    far = meta_of(jnp.where(y >= 2, 1, 0), 0)
    e0, at, flags, place, above, below_far, below_above, far = lax.optimization_barrier(
        (e0, at, flags, place, above, below_far, below_above, far)
    )
    e0_there = over_core(e0)
    e1 = over_dec(e0, 1)
    a0, b0 = over_y(e0, 1), over_y(e0, 3)
    e0_far, e0_there = lax.optimization_barrier((e0, e0_there))
    c0 = over_y(e0_far, 2)

    def near(z, meta, q, e, x, arrays=(), units=(), state=()):
        n = len(arrays)
        kv = [pltpu.VMEM((2 * len(units) * SEG, 2 * HD), jnp.bfloat16)] if units else []
        return call(
            functools.partial(near_kernel, z, units),
            meta,
            [q, e, x, *arrays, *state],
            [((tok, 2 * HD), jnp.bfloat16)] * (z == 0) + state_types,
            scratch_shapes=[pltpu.VMEM((SEG, 2 * HD), jnp.bfloat16), *kv],
            input_output_aliases={n + 4 + i: i for i in range(len(state))},
        )

    def more(meta, arrays, units, state, last=False):
        n = len(arrays)
        return call(
            functools.partial(next_kernel, n, units, last),
            meta,
            [q, *arrays, *state],
            state_types + [((tok, 2 * HD), jnp.bfloat16)] * last,
            scratch_shapes=[pltpu.VMEM((2 * len(units) * SEG, 2 * HD), jnp.bfloat16)],
            input_output_aliases={n + 2 + i: i for i in range(4)},
        )

    def both(first, second):
        return over_core(jnp.concatenate([first, second], axis=0))

    pair = [((0, 0),), ((1, 0),)]
    crossed = [((0, 0), (2, SEG)), ((2, 0),)]
    q, *state = near(0, place, queries, e0, e0_there)
    state = more(above, [a0, b0], [pair], state)
    a0, b0, c0, e1, state = lax.optimization_barrier((a0, b0, c0, e1, state))
    ab0_there = both(a0, b0)
    a1, b1 = over_y(e1, 1), over_y(e1, 3)
    e1_there, c0_there = over_core(e1), over_core(c0)
    e1_there, c0_there, state = lax.optimization_barrier((e1_there, c0_there, state))
    distant = [((3, 0),), ((4, 0),)]
    state = near(
        1,
        below_far,
        q,
        e1,
        e1_there,
        [a0, b0, ab0_there, c0, c0_there],
        [crossed, distant],
        state,
    )
    a1, b1, state = lax.optimization_barrier((a1, b1, state))
    ab1_there = both(a1, b1)
    half = SEG // 2
    c1 = over_y(a1[:half], 1), over_y(b1[half:], 3)
    state = more(below_above, [a1, b1, ab1_there], [crossed, pair], state)
    c1, state = lax.optimization_barrier((c1, state))
    c1 = jnp.concatenate(c1, axis=0)
    c1_there = over_core(c1)

    block = ((2 * PAGE, 2 * HD), jnp.bfloat16)
    at, state = lax.optimization_barrier((at, state))
    mine, to_head = call(
        pick_kernel,
        at,
        [e0, e1, b0, b1, c0, c1, a0, a1, e0_there, e1_there, c0_there, c1_there, ab0_there, ab1_there],
        [block] * 2,
    )
    state, mine = lax.optimization_barrier((state, mine))
    oth = over_dec(to_head, 4)
    *_, attended = more(far, [c1, c1_there], [pair], state, True)
    cache_keys, cache_values, key_scales, value_scales = call(
        cache_kernel,
        flags,
        [mine, oth],
        [block, block, ((2, 2), jnp.float32), ((2, 2), jnp.float32)],
    )
    return attended, cache_keys, cache_values, key_scales, value_scales


def solution(mesh):
    return jax.shard_map(
        body,
        mesh=mesh,
        in_specs=(
            P("blk", ("kvh", "dec")),
            P(("blk", "dec"), "kvh"),
            P(("blk", "dec"), "kvh"),
            P(),
        ),
        out_specs=(
            P("blk", ("kvh", "dec")),
            P(("blk", "dec"), "kvh"),
            P(("blk", "dec"), "kvh"),
            P(("blk", "dec"), "kvh"),
            P(("blk", "dec"), "kvh"),
        ),
        check_vma=False,
    )
```

```python
import functools

import jax
import jax.numpy as jnp
import numpy as np
from jax import lax
from jax.experimental import pallas as pl
from jax.experimental.pallas import tpu as pltpu
from jax.sharding import PartitionSpec as P

HEADS = 64
KVH = 8
HD = 128
PAGE = 128
TQ = 512
TN = 256
TS = 128
SEG = 512
C = float(np.log2(np.e) / np.sqrt(HD))
NEG = -1e30
LIMIT = 80.0
NT = (((1,), (1,)), ((), ()))


def longest(x):
    x = x.astype(jnp.float32)
    squares = jnp.dot(
        (x * x).astype(jnp.bfloat16),
        jnp.ones((HD, HD), jnp.bfloat16),
        preferred_element_type=jnp.float32,
    )
    return jnp.sqrt(jnp.max(squares))


def fast(q_ref, state, h, row, size, k, v, allowed=None):
    acc_ref, shift_ref, total_ref = state[:3]
    q = q_ref[rows_at(row, size), h * HD : (h + 1) * HD]
    r = rows_at(h * q_ref.shape[0] + row, size)
    s = lax.dot_general(q, k, NT, preferred_element_type=jnp.float32)
    p = jnp.exp2(s * C - shift_ref[r])
    if allowed is not None:
        p = jnp.where(allowed, p, 0.0)
    total_ref[r] += jnp.sum(p, axis=1, keepdims=True)
    acc_ref[r] += jnp.dot(p.astype(jnp.bfloat16), v, preferred_element_type=jnp.float32)


def slow(q_ref, state, h, row, size, k, v, allowed=True):
    acc_ref, shift_ref, total_ref = state[:3]
    q = q_ref[rows_at(row, size), h * HD : (h + 1) * HD]
    r = rows_at(h * q_ref.shape[0] + row, size)
    s = C * lax.dot_general(q, k, NT, preferred_element_type=jnp.float32)
    s = jnp.where(allowed, s, NEG)
    total = total_ref[r]
    old = jnp.where(total > 0, shift_ref[r], NEG)
    shift = jnp.maximum(old, jnp.max(s, axis=1, keepdims=True))
    p = jnp.where(allowed, jnp.exp2(s - shift), 0.0)
    a = jnp.exp2(old - shift)
    total = a * total + jnp.sum(p, axis=1, keepdims=True)
    shift_ref[r] = jnp.where(total > 0, shift, 0.0)
    total_ref[r] = total
    acc_ref[r] = a * acc_ref[r] + jnp.dot(
        p.astype(jnp.bfloat16), v, preferred_element_type=jnp.float32
    )


def loop(begin, end, step):
    def one(i, _):
        step(i)
        return 0

    lax.fori_loop(begin, end, one, 0)


def rows_at(start, size):
    return pl.ds(start if isinstance(start, int) else pl.multiple_of(start, size), size)


def guarded(state, key_norm, quick, careful):
    shift_ref, bound_ref = state[1], state[3]
    top = jnp.max(bound_ref[:, 0:1]) * key_norm * (1.02 * C) - jnp.min(bound_ref[:, 1:2])

    @pl.when(top <= LIMIT)
    def _():
        quick()

    @pl.when(jnp.logical_not(top <= LIMIT))
    def _():
        careful()
        lowest = jnp.minimum(jnp.min(shift_ref[...]), 0.0)
        bound_ref[:, 1:2] = jnp.full((8, 1), lowest)


def fill(meta, arrays, kv_ref, units):
    for u, unit in enumerate(units):
        for j, choices in enumerate(unit):
            for use, (i, row) in enumerate(choices):
                wanted = meta[0] > u
                if len(choices) > 1:
                    wanted = jnp.logical_and(wanted, meta[1] == use)

                @pl.when(wanted)
                def _():
                    at = (2 * u + j) * SEG
                    kv_ref[at : at + SEG] = arrays[i][row : row + SEG]


def norm_of(kv_ref, count):
    norms = [longest(kv_ref[at : at + 2 * SEG, :HD]) for at in range(0, kv_ref.shape[0], 2 * SEG)]
    norm = jnp.where(count > 0, norms[0], 0.0)
    for u in range(1, len(norms)):
        norm = jnp.maximum(norm, jnp.where(count > u, norms[u], 0.0))
    return norm


def units_quick(q_ref, state, kv_ref, count, finish=None):
    tiles = q_ref.shape[0] // (4 * TN)

    def step(i):
        keys = rows_at((i // tiles) * 2 * SEG, 2 * SEG)
        for part in range(4):
            row = (i % tiles) * 4 * TN + part * TN
            for h in range(2):
                fast(q_ref, state, h, row, TN, kv_ref[keys, :HD], kv_ref[keys, HD:])
                if finish is not None:
                    finish(h, row, TN)

    loop(0, count * tiles, step)


def units_careful(q_ref, state, kv_ref, count):
    few = q_ref.shape[0] // TS

    def step(i):
        keys = rows_at((i // few) * SEG, SEG)
        for h in range(2):
            slow(q_ref, state, h, (i % few) * TS, TS, kv_ref[keys, :HD], kv_ref[keys, HD:])

    loop(0, 2 * count * few, step)


def near_kernel(z, units, meta, q_ref, e_ref, x_ref, *refs):
    count = 0
    if units:
        kv_ref, arrays = refs[-1], refs[: len(refs) - 10]
        refs = refs[:-1]
        count = meta[0]
        fill(meta, arrays, kv_ref, units)
    state, page_ref = refs[-5:-1], refs[-1]
    acc_ref, shift_ref, total_ref, bound_ref = state
    rows = q_ref.shape[0]
    core, dec = meta[2], meta[3]
    if z == 0:
        refs[0][...] = q_ref[...]
        acc_ref[...] = jnp.zeros_like(acc_ref)
        shift_ref[...] = jnp.zeros_like(shift_ref)
        total_ref[...] = jnp.zeros_like(total_ref)
        bound_ref[...] = jnp.zeros_like(bound_ref)
        norm = jnp.maximum(longest(q_ref[:, :HD]), longest(q_ref[:, HD:]))
        bound_ref[:, 0:1] = jnp.full((8, 1), norm)
    parity = jnp.bitwise_xor(dec % 2, z)
    for i in range(SEG // PAGE):
        to = jnp.bitwise_xor(dec // 2, i) * PAGE
        page_ref[rows_at(to, PAGE)] = e_ref[i * PAGE : (i + 1) * PAGE]

    def quick():
        row = lax.broadcasted_iota(jnp.int32, (2 * PAGE, PAGE), 0)
        lane = lax.broadcasted_iota(jnp.int32, (2 * PAGE, PAGE), 1)
        last = parity * PAGE + lane <= row
        for t in range(SEG // PAGE):
            n = (t + 1) * PAGE
            allowed = last
            if t:
                allowed = jnp.concatenate([jnp.full((2 * PAGE, t * PAGE), True), last], axis=1)
            for h in range(2):
                fast(
                    q_ref,
                    state,
                    h,
                    t * 2 * PAGE,
                    2 * PAGE,
                    page_ref[:n, :HD],
                    page_ref[:n, HD:],
                    allowed,
                )

        def extra(i):
            for h in range(2):
                fast(q_ref, state, h, i * TQ, TQ, x_ref[:, :HD], x_ref[:, HD:])

        loop(0, jnp.where(core == 1, rows // TQ, 0), extra)
        if units:
            units_quick(q_ref, state, kv_ref, count)

    def careful():
        lane = lax.broadcasted_iota(jnp.int32, (1, SEG), 1)
        key_at = (2 * (lane // PAGE) + parity) * PAGE + lane % PAGE

        def diagonal(i):
            allowed = key_at <= i * TS + lax.broadcasted_iota(jnp.int32, (TS, 1), 0)
            for h in range(2):
                slow(q_ref, state, h, i * TS, TS, page_ref[:, :HD], page_ref[:, HD:], allowed)

        def extra(i):
            for h in range(2):
                slow(q_ref, state, h, i * TS, TS, x_ref[:, :HD], x_ref[:, HD:])

        loop(0, rows // TS, diagonal)
        loop(0, jnp.where(core == 1, rows // TS, 0), extra)
        if units:
            units_careful(q_ref, state, kv_ref, count)

    key_norm = jnp.maximum(longest(e_ref[:, :HD]), longest(x_ref[:, :HD]))
    if units:
        key_norm = jnp.maximum(key_norm, norm_of(kv_ref, count))
    guarded(state, key_norm, quick, careful)


def next_kernel(n, units, last, meta, q_ref, *refs):
    arrays = refs[:n]
    if last:
        state, out_ref, kv_ref = refs[-6:-2], *refs[-2:]
    else:
        state, kv_ref = refs[-5:-1], refs[-1]
    rows = q_ref.shape[0]
    count = meta[0]

    def finish(h, row, size):
        r = rows_at(h * rows + row, size)
        mean = state[0][r] * (1.0 / state[2][r])
        out_ref[rows_at(row, size), h * HD : (h + 1) * HD] = mean.astype(jnp.bfloat16)

    def finish_all():
        def step(i):
            for h in range(2):
                finish(h, i * TN, TN)

        loop(0, rows // TN, step)

    def careful():
        units_careful(q_ref, state, kv_ref, count)
        if last:
            finish_all()

    @pl.when(count > 0)
    def _():
        fill(meta, arrays, kv_ref, units)
        guarded(
            state,
            norm_of(kv_ref, count),
            lambda: units_quick(q_ref, state, kv_ref, count, finish if last else None),
            careful,
        )

    if last:
        pl.when(count == 0)(finish_all)


def pick_kernel(meta, *refs):
    pages, outs = refs[:-2], refs[-2:]
    own, (e0, e1, c0, c1, ab0, ab1) = pages[:8], pages[8:]
    places = [(ref, 0) for ref in (*own, e0, e1)]
    places += [(ab0, SEG), (ab1, SEG), (c0, 0), (c1, 0), (ab0, 0), (ab1, 0)]
    for d in range(2):
        for j in range(2):
            at = meta[2 * d + j]
            for b, (ref, start) in enumerate(places):

                @pl.when(at // 4 == b)
                def _():
                    rows = rows_at(start + (at % 4) * PAGE, PAGE)
                    outs[d][j * PAGE : (j + 1) * PAGE] = ref[rows]


def cache_kernel(meta, own, oth, ck, cv, ks, vs):
    col = meta[0]
    scales = [jnp.zeros((2, 2), jnp.float32)] * 2
    row_at = lax.broadcasted_iota(jnp.int32, (2, 2), 0)
    col_at = lax.broadcasted_iota(jnp.int32, (2, 2), 1)
    for j in range(2):
        filled = meta[1 + j] > 0
        rows = slice(j * PAGE, (j + 1) * PAGE)
        for kind, out in enumerate((ck, cv)):
            normed = []
            for b, block in enumerate((own, oth)):
                x = block[rows, kind * HD : (kind + 1) * HD].astype(jnp.float32)
                x = jnp.where(filled, x, 0.0)
                scale = jnp.max(jnp.abs(x), keepdims=True) + 1e-6
                normed.append((x / scale).astype(jnp.bfloat16))
                here = jnp.logical_and(row_at == j, col_at == (col if b == 0 else 1 - col))
                scales[kind] = jnp.where(jnp.logical_and(here, filled), scale, scales[kind])
            out[rows, :HD] = jnp.where(col == 0, normed[0], normed[1])
            out[rows, HD:] = jnp.where(col == 0, normed[1], normed[0])
    ks[...] = scales[0]
    vs[...] = scales[1]


VMEM = pl.BlockSpec(memory_space=pltpu.VMEM)
SMEM = pl.BlockSpec(memory_space=pltpu.SMEM)
PARAMS = pltpu.CompilerParams(vmem_limit_bytes=10 * 2**20)


def call(kernel, meta, arrays, outs, **more):
    return pl.pallas_call(
        kernel,
        in_specs=[SMEM] + [VMEM] * len(arrays),
        out_specs=[VMEM] * len(outs),
        out_shape=[jax.ShapeDtypeStruct(s, t) for s, t in outs],
        compiler_params=PARAMS,
        **more,
    )(meta, *arrays)


def body(queries, keys, values, page_slot):
    blk, dec = lax.axis_index("blk"), lax.axis_index("dec")
    y, core, head = blk // 2, blk % 2, dec // 4
    tok = queries.shape[0]
    i32 = jnp.int32

    def over_dec(x, m):
        return lax.ppermute(x, "dec", [(i, i ^ m) for i in range(8)])

    def over_core(x):
        return lax.ppermute(x, "blk", [(i, i ^ 1) for i in range(8)])

    def over_y(x, d):
        return lax.ppermute(x, "blk", [(i, (i + 2 * d) % 8) for i in range(8)])

    first = jnp.concatenate([keys[:, :HD], values[:, :HD]], axis=1)
    second = jnp.concatenate([keys[:, HD:], values[:, HD:]], axis=1)
    own = jnp.where(head == 0, first, second)
    other = jnp.where(head == 0, second, first)

    e0 = jnp.concatenate(
        [own, over_dec(own, 2), over_dec(other, 4), over_dec(other, 6)], axis=0
    )

    owners = jnp.stack([8 * blk + dec, 8 * blk + (dec ^ 4)])
    slots = (2 * owners[:, None] + jnp.arange(2)[None, :]).reshape(4)
    hits = page_slot[None, :] == slots[:, None]
    filled = jnp.any(hits, axis=1)
    page = jnp.sum(jnp.where(hits, jnp.arange(64)[None, :], 0), axis=1)
    page_blk, page_dec = page // 8, page % 8
    rel = page_dec ^ dec
    buffer = 8 * ((page_blk % 2) ^ core) + 2 * ((page_blk // 2 - y) % 4) + rel % 2
    at = jnp.where(filled, 4 * buffer + rel // 2, -1).astype(i32)
    flags = jnp.concatenate([head[None], filled[:2]]).astype(i32)

    state_types = [
        ((2 * tok, HD), jnp.float32),
        ((2 * tok, 1), jnp.float32),
        ((2 * tok, 1), jnp.float32),
        ((8, 2), jnp.float32),
    ]
    def meta_of(count, other):
        return jnp.stack([count + 0 * y, other + 0 * y, core, dec]).astype(i32)

    top = jnp.where(y == 3, 1, 0)
    some = jnp.where(y >= 1, 1, 0)
    place = meta_of(0, 0)
    above = meta_of(top, top)
    below_above = meta_of(some + top, top)
    below_far = meta_of(some + jnp.where(y >= 2, 1, 0), top)
    far = meta_of(jnp.where(y >= 2, 1, 0), 0)
    e0, at, flags, place, above, below_far, below_above, far = lax.optimization_barrier(
        (e0, at, flags, place, above, below_far, below_above, far)
    )
    e0_there = over_core(e0)
    e1 = over_dec(e0, 1)
    a0, b0 = over_y(e0, 1), over_y(e0, 3)
    e0_far, e0_there = lax.optimization_barrier((e0, e0_there))
    c0 = over_y(e0_far, 2)

    def near(z, meta, q, e, x, arrays=(), units=(), state=()):
        n = len(arrays)
        kv = [pltpu.VMEM((2 * len(units) * SEG, 2 * HD), jnp.bfloat16)] if units else []
        return call(
            functools.partial(near_kernel, z, units),
            meta,
            [q, e, x, *arrays, *state],
            [((tok, 2 * HD), jnp.bfloat16)] * (z == 0) + state_types,
            scratch_shapes=[pltpu.VMEM((SEG, 2 * HD), jnp.bfloat16), *kv],
            input_output_aliases={n + 4 + i: i for i in range(len(state))},
        )

    def more(meta, arrays, units, state, last=False):
        n = len(arrays)
        return call(
            functools.partial(next_kernel, n, units, last),
            meta,
            [q, *arrays, *state],
            state_types + [((tok, 2 * HD), jnp.bfloat16)] * last,
            scratch_shapes=[pltpu.VMEM((2 * len(units) * SEG, 2 * HD), jnp.bfloat16)],
            input_output_aliases={n + 2 + i: i for i in range(4)},
        )

    def both(first, second):
        return over_core(jnp.concatenate([first, second], axis=0))

    pair = [((0, 0),), ((1, 0),)]
    crossed = [((0, 0), (2, SEG)), ((2, 0),)]
    q, *state = near(0, place, queries, e0, e0_there)
    state = more(above, [a0, b0], [pair], state)
    a0, b0, c0, e1, state = lax.optimization_barrier((a0, b0, c0, e1, state))
    ab0_there = both(a0, b0)
    a1, b1 = over_y(e1, 1), over_y(e1, 3)
    e1_there, c0_there = over_core(e1), over_core(c0)
    e1_there, c0_there, state = lax.optimization_barrier((e1_there, c0_there, state))
    distant = [((3, 0),), ((4, 0),)]
    state = near(
        1,
        below_far,
        q,
        e1,
        e1_there,
        [a0, b0, ab0_there, c0, c0_there],
        [crossed, distant],
        state,
    )
    a1, b1, state = lax.optimization_barrier((a1, b1, state))
    ab1_there = both(a1, b1)
    half = SEG // 2
    c1 = over_y(a1[:half], 1), over_y(b1[half:], 3)
    state = more(below_above, [a1, b1, ab1_there], [crossed, pair], state)
    c1, state = lax.optimization_barrier((c1, state))
    c1 = jnp.concatenate(c1, axis=0)
    c1_there = over_core(c1)

    block = ((2 * PAGE, 2 * HD), jnp.bfloat16)
    at, state = lax.optimization_barrier((at, state))
    mine, to_head = call(
        pick_kernel,
        at,
        [e0, e1, b0, b1, c0, c1, a0, a1, e0_there, e1_there, c0_there, c1_there, ab0_there, ab1_there],
        [block] * 2,
    )
    state, mine = lax.optimization_barrier((state, mine))
    oth = over_dec(to_head, 4)
    *_, attended = more(far, [c1, c1_there], [pair], state, True)
    cache_keys, cache_values, key_scales, value_scales = call(
        cache_kernel,
        flags,
        [mine, oth],
        [block, block, ((2, 2), jnp.float32), ((2, 2), jnp.float32)],
    )
    return attended, cache_keys, cache_values, key_scales, value_scales


def solution(mesh):
    return jax.shard_map(
        body,
        mesh=mesh,
        in_specs=(
            P("blk", ("kvh", "dec")),
            P(("blk", "dec"), "kvh"),
            P(("blk", "dec"), "kvh"),
            P(),
        ),
        out_specs=(
            P("blk", ("kvh", "dec")),
            P(("blk", "dec"), "kvh"),
            P(("blk", "dec"), "kvh"),
            P(("blk", "dec"), "kvh"),
            P(("blk", "dec"), "kvh"),
        ),
        check_vma=False,
    )
```

```python
import functools

import jax
import jax.numpy as jnp
import numpy as np
from jax import lax
from jax.experimental import pallas as pl
from jax.experimental.pallas import tpu as pltpu
from jax.sharding import PartitionSpec as P

HEADS = 64
KVH = 8
HD = 128
PAGE = 128
TQ = 512
TN = 256
TS = 128
SEG = 512
C = float(np.log2(np.e) / np.sqrt(HD))
NEG = -1e30
LIMIT = 80.0
NT = (((1,), (1,)), ((), ()))


def longest(x):
    x = x.astype(jnp.float32)
    squares = jnp.dot(
        (x * x).astype(jnp.bfloat16),
        jnp.ones((HD, HD), jnp.bfloat16),
        preferred_element_type=jnp.float32,
    )
    return jnp.sqrt(jnp.max(squares))


def fast(q_ref, state, h, row, size, k, v, allowed=None):
    acc_ref, shift_ref, total_ref = state[:3]
    q = q_ref[rows_at(row, size), h * HD : (h + 1) * HD]
    r = rows_at(h * q_ref.shape[0] + row, size)
    s = lax.dot_general(q, k, NT, preferred_element_type=jnp.float32)
    p = jnp.exp2(s * C - shift_ref[r])
    if allowed is not None:
        p = jnp.where(allowed, p, 0.0)
    total_ref[r] += jnp.sum(p, axis=1, keepdims=True)
    acc_ref[r] += jnp.dot(p.astype(jnp.bfloat16), v, preferred_element_type=jnp.float32)


def slow(q_ref, state, h, row, size, k, v, allowed=True):
    acc_ref, shift_ref, total_ref = state[:3]
    q = q_ref[rows_at(row, size), h * HD : (h + 1) * HD]
    r = rows_at(h * q_ref.shape[0] + row, size)
    s = C * lax.dot_general(q, k, NT, preferred_element_type=jnp.float32)
    s = jnp.where(allowed, s, NEG)
    total = total_ref[r]
    old = jnp.where(total > 0, shift_ref[r], NEG)
    shift = jnp.maximum(old, jnp.max(s, axis=1, keepdims=True))
    p = jnp.where(allowed, jnp.exp2(s - shift), 0.0)
    a = jnp.exp2(old - shift)
    total = a * total + jnp.sum(p, axis=1, keepdims=True)
    shift_ref[r] = jnp.where(total > 0, shift, 0.0)
    total_ref[r] = total
    acc_ref[r] = a * acc_ref[r] + jnp.dot(
        p.astype(jnp.bfloat16), v, preferred_element_type=jnp.float32
    )


def loop(begin, end, step):
    def one(i, _):
        step(i)
        return 0

    lax.fori_loop(begin, end, one, 0)


def rows_at(start, size):
    return pl.ds(start if isinstance(start, int) else pl.multiple_of(start, size), size)


def guarded(state, key_norm, quick, careful):
    shift_ref, bound_ref = state[1], state[3]
    top = jnp.max(bound_ref[:, 0:1]) * key_norm * (1.02 * C) - jnp.min(bound_ref[:, 1:2])

    @pl.when(top <= LIMIT)
    def _():
        quick()

    @pl.when(jnp.logical_not(top <= LIMIT))
    def _():
        careful()
        lowest = jnp.minimum(jnp.min(shift_ref[...]), 0.0)
        bound_ref[:, 1:2] = jnp.full((8, 1), lowest)


def fill(meta, arrays, kv_ref, units):
    for u, unit in enumerate(units):
        for j, choices in enumerate(unit):
            for use, (i, row) in enumerate(choices):
                wanted = meta[0] > u
                if len(choices) > 1:
                    wanted = jnp.logical_and(wanted, meta[1] == use)

                @pl.when(wanted)
                def _():
                    at = (2 * u + j) * SEG
                    kv_ref[at : at + SEG] = arrays[i][row : row + SEG]


def norm_of(kv_ref, count):
    norms = [longest(kv_ref[at : at + 2 * SEG, :HD]) for at in range(0, kv_ref.shape[0], 2 * SEG)]
    norm = jnp.where(count > 0, norms[0], 0.0)
    for u in range(1, len(norms)):
        norm = jnp.maximum(norm, jnp.where(count > u, norms[u], 0.0))
    return norm


def units_quick(q_ref, state, kv_ref, count, finish=None):
    tiles = q_ref.shape[0] // (4 * TN)

    def step(i):
        keys = rows_at((i // tiles) * 2 * SEG, 2 * SEG)
        for part in range(4):
            row = (i % tiles) * 4 * TN + part * TN
            for h in range(2):
                fast(q_ref, state, h, row, TN, kv_ref[keys, :HD], kv_ref[keys, HD:])
                if finish is not None:
                    finish(h, row, TN)

    loop(0, count * tiles, step)


def units_careful(q_ref, state, kv_ref, count):
    few = q_ref.shape[0] // TS

    def step(i):
        keys = rows_at((i // few) * SEG, SEG)
        for h in range(2):
            slow(q_ref, state, h, (i % few) * TS, TS, kv_ref[keys, :HD], kv_ref[keys, HD:])

    loop(0, 2 * count * few, step)


def near_kernel(z, units, meta, q_ref, e_ref, x_ref, *refs):
    count = 0
    if units:
        kv_ref, arrays = refs[-1], refs[: len(refs) - 10]
        refs = refs[:-1]
        count = meta[0]
        fill(meta, arrays, kv_ref, units)
    state, page_ref = refs[-5:-1], refs[-1]
    acc_ref, shift_ref, total_ref, bound_ref = state
    rows = q_ref.shape[0]
    core, dec = meta[2], meta[3]
    if z == 0:
        refs[0][...] = q_ref[...]
        acc_ref[...] = jnp.zeros_like(acc_ref)
        shift_ref[...] = jnp.zeros_like(shift_ref)
        total_ref[...] = jnp.zeros_like(total_ref)
        bound_ref[...] = jnp.zeros_like(bound_ref)
        norm = jnp.maximum(longest(q_ref[:, :HD]), longest(q_ref[:, HD:]))
        bound_ref[:, 0:1] = jnp.full((8, 1), norm)
    parity = jnp.bitwise_xor(dec % 2, z)
    for i in range(SEG // PAGE):
        to = jnp.bitwise_xor(dec // 2, i) * PAGE
        page_ref[rows_at(to, PAGE)] = e_ref[i * PAGE : (i + 1) * PAGE]

    def quick():
        row = lax.broadcasted_iota(jnp.int32, (2 * PAGE, PAGE), 0)
        lane = lax.broadcasted_iota(jnp.int32, (2 * PAGE, PAGE), 1)
        last = parity * PAGE + lane <= row
        for t in range(SEG // PAGE):
            n = (t + 1) * PAGE
            allowed = last
            if t:
                allowed = jnp.concatenate([jnp.full((2 * PAGE, t * PAGE), True), last], axis=1)
            for h in range(2):
                fast(
                    q_ref,
                    state,
                    h,
                    t * 2 * PAGE,
                    2 * PAGE,
                    page_ref[:n, :HD],
                    page_ref[:n, HD:],
                    allowed,
                )

        def extra(i):
            for h in range(2):
                fast(q_ref, state, h, i * TQ, TQ, x_ref[:, :HD], x_ref[:, HD:])

        loop(0, jnp.where(core == 1, rows // TQ, 0), extra)
        if units:
            units_quick(q_ref, state, kv_ref, count)

    def careful():
        lane = lax.broadcasted_iota(jnp.int32, (1, SEG), 1)
        key_at = (2 * (lane // PAGE) + parity) * PAGE + lane % PAGE

        def diagonal(i):
            allowed = key_at <= i * TS + lax.broadcasted_iota(jnp.int32, (TS, 1), 0)
            for h in range(2):
                slow(q_ref, state, h, i * TS, TS, page_ref[:, :HD], page_ref[:, HD:], allowed)

        def extra(i):
            for h in range(2):
                slow(q_ref, state, h, i * TS, TS, x_ref[:, :HD], x_ref[:, HD:])

        loop(0, rows // TS, diagonal)
        loop(0, jnp.where(core == 1, rows // TS, 0), extra)
        if units:
            units_careful(q_ref, state, kv_ref, count)

    key_norm = jnp.maximum(longest(e_ref[:, :HD]), longest(x_ref[:, :HD]))
    if units:
        key_norm = jnp.maximum(key_norm, norm_of(kv_ref, count))
    guarded(state, key_norm, quick, careful)


def next_kernel(n, units, last, meta, q_ref, *refs):
    arrays = refs[:n]
    if last:
        state, out_ref, kv_ref = refs[-6:-2], *refs[-2:]
    else:
        state, kv_ref = refs[-5:-1], refs[-1]
    rows = q_ref.shape[0]
    count = meta[0]

    def finish(h, row, size):
        r = rows_at(h * rows + row, size)
        mean = state[0][r] * (1.0 / state[2][r])
        out_ref[rows_at(row, size), h * HD : (h + 1) * HD] = mean.astype(jnp.bfloat16)

    def finish_all():
        def step(i):
            for h in range(2):
                finish(h, i * TN, TN)

        loop(0, rows // TN, step)

    def careful():
        units_careful(q_ref, state, kv_ref, count)
        if last:
            finish_all()

    @pl.when(count > 0)
    def _():
        fill(meta, arrays, kv_ref, units)
        guarded(
            state,
            norm_of(kv_ref, count),
            lambda: units_quick(q_ref, state, kv_ref, count, finish if last else None),
            careful,
        )

    if last:
        pl.when(count == 0)(finish_all)


def pick_kernel(meta, *refs):
    pages, outs = refs[:-2], refs[-2:]
    own, (e0, e1, c0, c1, ab0, ab1) = pages[:8], pages[8:]
    places = [(ref, 0) for ref in (*own, e0, e1)]
    places += [(ab0, SEG), (ab1, SEG), (c0, 0), (c1, 0), (ab0, 0), (ab1, 0)]
    def copy(out, j, at):
        for group in range(0, len(places), 4):

            @pl.when(at // 16 == group // 4)
            def _():
                for b in range(group, group + 4):
                    ref, start = places[b]

                    @pl.when(at // 4 == b)
                    def _():
                        rows = rows_at(start + (at % 4) * PAGE, PAGE)
                        out[j * PAGE : (j + 1) * PAGE] = ref[rows]

    for d in range(2):
        for j in range(2):
            copy(outs[d], j, meta[2 * d + j])


def cache_kernel(meta, own, oth, ck, cv, ks, vs):
    col = meta[0]
    scales = [jnp.zeros((2, 2), jnp.float32)] * 2
    row_at = lax.broadcasted_iota(jnp.int32, (2, 2), 0)
    col_at = lax.broadcasted_iota(jnp.int32, (2, 2), 1)
    for j in range(2):
        filled = meta[1 + j] > 0
        rows = slice(j * PAGE, (j + 1) * PAGE)
        for kind, out in enumerate((ck, cv)):
            normed = []
            for b, block in enumerate((own, oth)):
                x = block[rows, kind * HD : (kind + 1) * HD].astype(jnp.float32)
                x = jnp.where(filled, x, 0.0)
                scale = jnp.max(jnp.abs(x), keepdims=True) + 1e-6
                normed.append((x / scale).astype(jnp.bfloat16))
                here = jnp.logical_and(row_at == j, col_at == (col if b == 0 else 1 - col))
                scales[kind] = jnp.where(jnp.logical_and(here, filled), scale, scales[kind])
            out[rows, :HD] = jnp.where(col == 0, normed[0], normed[1])
            out[rows, HD:] = jnp.where(col == 0, normed[1], normed[0])
    ks[...] = scales[0]
    vs[...] = scales[1]


VMEM = pl.BlockSpec(memory_space=pltpu.VMEM)
SMEM = pl.BlockSpec(memory_space=pltpu.SMEM)
PARAMS = pltpu.CompilerParams(vmem_limit_bytes=10 * 2**20)


def call(kernel, meta, arrays, outs, **more):
    return pl.pallas_call(
        kernel,
        in_specs=[SMEM] + [VMEM] * len(arrays),
        out_specs=[VMEM] * len(outs),
        out_shape=[jax.ShapeDtypeStruct(s, t) for s, t in outs],
        compiler_params=PARAMS,
        **more,
    )(meta, *arrays)


def body(queries, keys, values, page_slot):
    blk, dec = lax.axis_index("blk"), lax.axis_index("dec")
    y, core, head = blk // 2, blk % 2, dec // 4
    tok = queries.shape[0]
    i32 = jnp.int32

    def over_dec(x, m):
        return lax.ppermute(x, "dec", [(i, i ^ m) for i in range(8)])

    def over_core(x):
        return lax.ppermute(x, "blk", [(i, i ^ 1) for i in range(8)])

    def over_y(x, d):
        return lax.ppermute(x, "blk", [(i, (i + 2 * d) % 8) for i in range(8)])

    first = jnp.concatenate([keys[:, :HD], values[:, :HD]], axis=1)
    second = jnp.concatenate([keys[:, HD:], values[:, HD:]], axis=1)
    own = jnp.where(head == 0, first, second)
    other = jnp.where(head == 0, second, first)

    e0 = jnp.concatenate(
        [own, over_dec(own, 2), over_dec(other, 4), over_dec(other, 6)], axis=0
    )

    owners = jnp.stack([8 * blk + dec, 8 * blk + (dec ^ 4)])
    slots = (2 * owners[:, None] + jnp.arange(2)[None, :]).reshape(4)
    hits = page_slot[None, :] == slots[:, None]
    filled = jnp.any(hits, axis=1)
    page = jnp.sum(jnp.where(hits, jnp.arange(64)[None, :], 0), axis=1)
    page_blk, page_dec = page // 8, page % 8
    rel = page_dec ^ dec
    buffer = 8 * ((page_blk % 2) ^ core) + 2 * ((page_blk // 2 - y) % 4) + rel % 2
    at = jnp.where(filled, 4 * buffer + rel // 2, -1).astype(i32)
    flags = jnp.concatenate([head[None], filled[:2]]).astype(i32)

    state_types = [
        ((2 * tok, HD), jnp.float32),
        ((2 * tok, 1), jnp.float32),
        ((2 * tok, 1), jnp.float32),
        ((8, 2), jnp.float32),
    ]
    def meta_of(count, other):
        return jnp.stack([count + 0 * y, other + 0 * y, core, dec]).astype(i32)

    top = jnp.where(y == 3, 1, 0)
    some = jnp.where(y >= 1, 1, 0)
    place = meta_of(0, 0)
    above = meta_of(top, top)
    below_above = meta_of(some + top, top)
    below_far = meta_of(some + jnp.where(y >= 2, 1, 0), top)
    far = meta_of(jnp.where(y >= 2, 1, 0), 0)
    e0, at, flags, place, above, below_far, below_above, far = lax.optimization_barrier(
        (e0, at, flags, place, above, below_far, below_above, far)
    )
    e0_there = over_core(e0)
    e1 = over_dec(e0, 1)
    a0, b0 = over_y(e0, 1), over_y(e0, 3)
    e0_far, e0_there = lax.optimization_barrier((e0, e0_there))
    c0 = over_y(e0_far, 2)

    def near(z, meta, q, e, x, arrays=(), units=(), state=()):
        n = len(arrays)
        kv = [pltpu.VMEM((2 * len(units) * SEG, 2 * HD), jnp.bfloat16)] if units else []
        return call(
            functools.partial(near_kernel, z, units),
            meta,
            [q, e, x, *arrays, *state],
            [((tok, 2 * HD), jnp.bfloat16)] * (z == 0) + state_types,
            scratch_shapes=[pltpu.VMEM((SEG, 2 * HD), jnp.bfloat16), *kv],
            input_output_aliases={n + 4 + i: i for i in range(len(state))},
        )

    def more(meta, arrays, units, state, last=False):
        n = len(arrays)
        return call(
            functools.partial(next_kernel, n, units, last),
            meta,
            [q, *arrays, *state],
            state_types + [((tok, 2 * HD), jnp.bfloat16)] * last,
            scratch_shapes=[pltpu.VMEM((2 * len(units) * SEG, 2 * HD), jnp.bfloat16)],
            input_output_aliases={n + 2 + i: i for i in range(4)},
        )

    def both(first, second):
        return over_core(jnp.concatenate([first, second], axis=0))

    pair = [((0, 0),), ((1, 0),)]
    crossed = [((0, 0), (2, SEG)), ((2, 0),)]
    q, *state = near(0, place, queries, e0, e0_there)
    state = more(above, [a0, b0], [pair], state)
    a0, b0, c0, e1, state = lax.optimization_barrier((a0, b0, c0, e1, state))
    ab0_there = both(a0, b0)
    a1, b1 = over_y(e1, 1), over_y(e1, 3)
    e1_there, c0_there = over_core(e1), over_core(c0)
    e1_there, c0_there, state = lax.optimization_barrier((e1_there, c0_there, state))
    distant = [((3, 0),), ((4, 0),)]
    state = near(
        1,
        below_far,
        q,
        e1,
        e1_there,
        [a0, b0, ab0_there, c0, c0_there],
        [crossed, distant],
        state,
    )
    a1, b1, state = lax.optimization_barrier((a1, b1, state))
    ab1_there = both(a1, b1)
    half = SEG // 2
    c1 = over_y(a1[:half], 1), over_y(b1[half:], 3)
    state = more(below_above, [a1, b1, ab1_there], [crossed, pair], state)
    c1, state = lax.optimization_barrier((c1, state))
    c1 = jnp.concatenate(c1, axis=0)
    c1_there = over_core(c1)

    block = ((2 * PAGE, 2 * HD), jnp.bfloat16)
    at, state = lax.optimization_barrier((at, state))
    mine, to_head = call(
        pick_kernel,
        at,
        [e0, e1, b0, b1, c0, c1, a0, a1, e0_there, e1_there, c0_there, c1_there, ab0_there, ab1_there],
        [block] * 2,
    )
    state, mine = lax.optimization_barrier((state, mine))
    oth = over_dec(to_head, 4)
    *_, attended = more(far, [c1, c1_there], [pair], state, True)
    cache_keys, cache_values, key_scales, value_scales = call(
        cache_kernel,
        flags,
        [mine, oth],
        [block, block, ((2, 2), jnp.float32), ((2, 2), jnp.float32)],
    )
    return attended, cache_keys, cache_values, key_scales, value_scales


def solution(mesh):
    return jax.shard_map(
        body,
        mesh=mesh,
        in_specs=(
            P("blk", ("kvh", "dec")),
            P(("blk", "dec"), "kvh"),
            P(("blk", "dec"), "kvh"),
            P(),
        ),
        out_specs=(
            P("blk", ("kvh", "dec")),
            P(("blk", "dec"), "kvh"),
            P(("blk", "dec"), "kvh"),
            P(("blk", "dec"), "kvh"),
            P(("blk", "dec"), "kvh"),
        ),
        check_vma=False,
    )
```

```python
import functools

import jax
import jax.numpy as jnp
import numpy as np
from jax import lax
from jax.experimental import pallas as pl
from jax.experimental.pallas import tpu as pltpu
from jax.sharding import PartitionSpec as P

HEADS = 64
KVH = 8
HD = 128
PAGE = 128
TQ = 512
TN = 256
TS = 128
SEG = 512
C = float(np.log2(np.e) / np.sqrt(HD))
NEG = -1e30
LIMIT = 80.0
NT = (((1,), (1,)), ((), ()))


def longest(x):
    squares = jnp.dot(
        x * x,
        jnp.ones((HD, HD), jnp.bfloat16),
        preferred_element_type=jnp.float32,
    )
    return jnp.sqrt(jnp.max(squares))


def fast(q_ref, state, h, row, size, k, v, allowed=None):
    acc_ref, shift_ref, total_ref = state[:3]
    q = q_ref[rows_at(row, size), h * HD : (h + 1) * HD]
    r = rows_at(h * q_ref.shape[0] + row, size)
    s = lax.dot_general(q, k, NT, preferred_element_type=jnp.float32)
    p = jnp.exp2(s * C - shift_ref[r])
    if allowed is not None:
        p = jnp.where(allowed, p, 0.0)
    total_ref[r] += jnp.sum(p, axis=1, keepdims=True)
    acc_ref[r] += jnp.dot(p.astype(jnp.bfloat16), v, preferred_element_type=jnp.float32)


def slow(q_ref, state, h, row, size, k, v, allowed=True):
    acc_ref, shift_ref, total_ref = state[:3]
    q = q_ref[rows_at(row, size), h * HD : (h + 1) * HD]
    r = rows_at(h * q_ref.shape[0] + row, size)
    s = C * lax.dot_general(q, k, NT, preferred_element_type=jnp.float32)
    s = jnp.where(allowed, s, NEG)
    total = total_ref[r]
    old = jnp.where(total > 0, shift_ref[r], NEG)
    shift = jnp.maximum(old, jnp.max(s, axis=1, keepdims=True))
    p = jnp.where(allowed, jnp.exp2(s - shift), 0.0)
    a = jnp.exp2(old - shift)
    total = a * total + jnp.sum(p, axis=1, keepdims=True)
    shift_ref[r] = jnp.where(total > 0, shift, 0.0)
    total_ref[r] = total
    acc_ref[r] = a * acc_ref[r] + jnp.dot(
        p.astype(jnp.bfloat16), v, preferred_element_type=jnp.float32
    )


def loop(begin, end, step):
    def one(i, _):
        step(i)
        return 0

    lax.fori_loop(begin, end, one, 0)


def rows_at(start, size):
    return pl.ds(start if isinstance(start, int) else pl.multiple_of(start, size), size)


def guarded(state, key_norm, quick, careful):
    shift_ref, bound_ref = state[1], state[3]
    top = jnp.max(bound_ref[:, 0:1]) * key_norm * (1.02 * C) - jnp.min(bound_ref[:, 1:2])

    @pl.when(top <= LIMIT)
    def _():
        quick()

    @pl.when(jnp.logical_not(top <= LIMIT))
    def _():
        careful()
        lowest = jnp.minimum(jnp.min(shift_ref[...]), 0.0)
        bound_ref[:, 1:2] = jnp.full((8, 1), lowest)


def fill(meta, arrays, kv_ref, units):
    for u, unit in enumerate(units):
        for j, choices in enumerate(unit):
            for use, (i, row) in enumerate(choices):
                wanted = meta[0] > u
                if len(choices) > 1:
                    wanted = jnp.logical_and(wanted, meta[1] == use)

                @pl.when(wanted)
                def _():
                    at = (2 * u + j) * SEG
                    kv_ref[at : at + SEG] = arrays[i][row : row + SEG]


def norm_of(kv_ref, count):
    norms = [longest(kv_ref[at : at + 2 * SEG, :HD]) for at in range(0, kv_ref.shape[0], 2 * SEG)]
    norm = jnp.where(count > 0, norms[0], 0.0)
    for u in range(1, len(norms)):
        norm = jnp.maximum(norm, jnp.where(count > u, norms[u], 0.0))
    return norm


def units_quick(q_ref, state, kv_ref, count, finish=None):
    tiles = q_ref.shape[0] // (4 * TN)

    def step(i):
        keys = rows_at((i // tiles) * 2 * SEG, 2 * SEG)
        for part in range(4):
            row = (i % tiles) * 4 * TN + part * TN
            for h in range(2):
                fast(q_ref, state, h, row, TN, kv_ref[keys, :HD], kv_ref[keys, HD:])
                if finish is not None:
                    finish(h, row, TN)

    loop(0, count * tiles, step)


def units_careful(q_ref, state, kv_ref, count):
    few = q_ref.shape[0] // TS

    def step(i):
        keys = rows_at((i // few) * SEG, SEG)
        for h in range(2):
            slow(q_ref, state, h, (i % few) * TS, TS, kv_ref[keys, :HD], kv_ref[keys, HD:])

    loop(0, 2 * count * few, step)


def near_kernel(z, units, meta, q_ref, e_ref, x_ref, *refs):
    count = 0
    if units:
        kv_ref, arrays = refs[-1], refs[: len(refs) - 10]
        refs = refs[:-1]
        count = meta[0]
        fill(meta, arrays, kv_ref, units)
    state, page_ref = refs[-5:-1], refs[-1]
    acc_ref, shift_ref, total_ref, bound_ref = state
    rows = q_ref.shape[0]
    core, dec = meta[2], meta[3]
    if z == 0:
        refs[0][...] = q_ref[...]
        acc_ref[...] = jnp.zeros_like(acc_ref)
        shift_ref[...] = jnp.zeros_like(shift_ref)
        total_ref[...] = jnp.zeros_like(total_ref)
        bound_ref[...] = jnp.zeros_like(bound_ref)
        norm = jnp.maximum(longest(q_ref[:, :HD]), longest(q_ref[:, HD:]))
        bound_ref[:, 0:1] = jnp.full((8, 1), norm)
    parity = jnp.bitwise_xor(dec % 2, z)
    for i in range(SEG // PAGE):
        to = jnp.bitwise_xor(dec // 2, i) * PAGE
        page_ref[rows_at(to, PAGE)] = e_ref[i * PAGE : (i + 1) * PAGE]

    def quick():
        row = lax.broadcasted_iota(jnp.int32, (2 * PAGE, PAGE), 0)
        lane = lax.broadcasted_iota(jnp.int32, (2 * PAGE, PAGE), 1)
        last = parity * PAGE + lane <= row
        for t in range(SEG // PAGE):
            n = (t + 1) * PAGE
            allowed = last
            if t:
                allowed = jnp.concatenate([jnp.full((2 * PAGE, t * PAGE), True), last], axis=1)
            for h in range(2):
                fast(
                    q_ref,
                    state,
                    h,
                    t * 2 * PAGE,
                    2 * PAGE,
                    page_ref[:n, :HD],
                    page_ref[:n, HD:],
                    allowed,
                )

        def extra(i):
            for h in range(2):
                fast(q_ref, state, h, i * TQ, TQ, x_ref[:, :HD], x_ref[:, HD:])

        loop(0, jnp.where(core == 1, rows // TQ, 0), extra)
        if units:
            units_quick(q_ref, state, kv_ref, count)

    def careful():
        lane = lax.broadcasted_iota(jnp.int32, (1, SEG), 1)
        key_at = (2 * (lane // PAGE) + parity) * PAGE + lane % PAGE

        def diagonal(i):
            allowed = key_at <= i * TS + lax.broadcasted_iota(jnp.int32, (TS, 1), 0)
            for h in range(2):
                slow(q_ref, state, h, i * TS, TS, page_ref[:, :HD], page_ref[:, HD:], allowed)

        def extra(i):
            for h in range(2):
                slow(q_ref, state, h, i * TS, TS, x_ref[:, :HD], x_ref[:, HD:])

        loop(0, rows // TS, diagonal)
        loop(0, jnp.where(core == 1, rows // TS, 0), extra)
        if units:
            units_careful(q_ref, state, kv_ref, count)

    key_norm = jnp.maximum(longest(e_ref[:, :HD]), longest(x_ref[:, :HD]))
    if units:
        key_norm = jnp.maximum(key_norm, norm_of(kv_ref, count))
    guarded(state, key_norm, quick, careful)


def next_kernel(n, units, last, meta, q_ref, *refs):
    arrays = refs[:n]
    if last:
        state, out_ref, kv_ref = refs[-6:-2], *refs[-2:]
    else:
        state, kv_ref = refs[-5:-1], refs[-1]
    rows = q_ref.shape[0]
    count = meta[0]

    def finish(h, row, size):
        r = rows_at(h * rows + row, size)
        mean = state[0][r] * (1.0 / state[2][r])
        out_ref[rows_at(row, size), h * HD : (h + 1) * HD] = mean.astype(jnp.bfloat16)

    def finish_all():
        def step(i):
            for h in range(2):
                finish(h, i * TN, TN)

        loop(0, rows // TN, step)

    def careful():
        units_careful(q_ref, state, kv_ref, count)
        if last:
            finish_all()

    @pl.when(count > 0)
    def _():
        fill(meta, arrays, kv_ref, units)
        guarded(
            state,
            norm_of(kv_ref, count),
            lambda: units_quick(q_ref, state, kv_ref, count, finish if last else None),
            careful,
        )

    if last:
        pl.when(count == 0)(finish_all)


def pick_kernel(meta, *refs):
    pages, outs = refs[:-2], refs[-2:]
    own, (e0, e1, c0, c1, ab0, ab1) = pages[:8], pages[8:]
    places = [(ref, 0) for ref in (*own, e0, e1)]
    places += [(ab0, SEG), (ab1, SEG), (c0, 0), (c1, 0), (ab0, 0), (ab1, 0)]
    def copy(out, j, at):
        for group in range(0, len(places), 4):

            @pl.when(at // 16 == group // 4)
            def _():
                for b in range(group, group + 4):
                    ref, start = places[b]

                    @pl.when(at // 4 == b)
                    def _():
                        rows = rows_at(start + (at % 4) * PAGE, PAGE)
                        out[j * PAGE : (j + 1) * PAGE] = ref[rows]

    for d in range(2):
        for j in range(2):
            copy(outs[d], j, meta[2 * d + j])


def cache_kernel(meta, own, oth, ck, cv, ks, vs):
    col = meta[0]
    scales = [jnp.zeros((2, 2), jnp.float32)] * 2
    row_at = lax.broadcasted_iota(jnp.int32, (2, 2), 0)
    col_at = lax.broadcasted_iota(jnp.int32, (2, 2), 1)
    for j in range(2):
        filled = meta[1 + j] > 0
        rows = slice(j * PAGE, (j + 1) * PAGE)
        for kind, out in enumerate((ck, cv)):
            normed = []
            for b, block in enumerate((own, oth)):
                x = block[rows, kind * HD : (kind + 1) * HD].astype(jnp.float32)
                x = jnp.where(filled, x, 0.0)
                scale = jnp.max(jnp.abs(x), keepdims=True) + 1e-6
                normed.append((x / scale).astype(jnp.bfloat16))
                here = jnp.logical_and(row_at == j, col_at == (col if b == 0 else 1 - col))
                scales[kind] = jnp.where(jnp.logical_and(here, filled), scale, scales[kind])
            out[rows, :HD] = jnp.where(col == 0, normed[0], normed[1])
            out[rows, HD:] = jnp.where(col == 0, normed[1], normed[0])
    ks[...] = scales[0]
    vs[...] = scales[1]


VMEM = pl.BlockSpec(memory_space=pltpu.VMEM)
SMEM = pl.BlockSpec(memory_space=pltpu.SMEM)
PARAMS = pltpu.CompilerParams(vmem_limit_bytes=10 * 2**20)


def call(kernel, meta, arrays, outs, **more):
    return pl.pallas_call(
        kernel,
        in_specs=[SMEM] + [VMEM] * len(arrays),
        out_specs=[VMEM] * len(outs),
        out_shape=[jax.ShapeDtypeStruct(s, t) for s, t in outs],
        compiler_params=PARAMS,
        **more,
    )(meta, *arrays)


def body(queries, keys, values, page_slot):
    blk, dec = lax.axis_index("blk"), lax.axis_index("dec")
    y, core, head = blk // 2, blk % 2, dec // 4
    tok = queries.shape[0]
    i32 = jnp.int32

    def over_dec(x, m):
        return lax.ppermute(x, "dec", [(i, i ^ m) for i in range(8)])

    def over_core(x):
        return lax.ppermute(x, "blk", [(i, i ^ 1) for i in range(8)])

    def over_y(x, d):
        return lax.ppermute(x, "blk", [(i, (i + 2 * d) % 8) for i in range(8)])

    first = jnp.concatenate([keys[:, :HD], values[:, :HD]], axis=1)
    second = jnp.concatenate([keys[:, HD:], values[:, HD:]], axis=1)
    own = jnp.where(head == 0, first, second)
    other = jnp.where(head == 0, second, first)

    e0 = jnp.concatenate(
        [own, over_dec(own, 2), over_dec(other, 4), over_dec(other, 6)], axis=0
    )

    owners = jnp.stack([8 * blk + dec, 8 * blk + (dec ^ 4)])
    slots = (2 * owners[:, None] + jnp.arange(2)[None, :]).reshape(4)
    hits = page_slot[None, :] == slots[:, None]
    filled = jnp.any(hits, axis=1)
    page = jnp.sum(jnp.where(hits, jnp.arange(64)[None, :], 0), axis=1)
    page_blk, page_dec = page // 8, page % 8
    rel = page_dec ^ dec
    buffer = 8 * ((page_blk % 2) ^ core) + 2 * ((page_blk // 2 - y) % 4) + rel % 2
    at = jnp.where(filled, 4 * buffer + rel // 2, -1).astype(i32)
    flags = jnp.concatenate([head[None], filled[:2]]).astype(i32)

    state_types = [
        ((2 * tok, HD), jnp.float32),
        ((2 * tok, 1), jnp.float32),
        ((2 * tok, 1), jnp.float32),
        ((8, 2), jnp.float32),
    ]
    def meta_of(count, other):
        return jnp.stack([count + 0 * y, other + 0 * y, core, dec]).astype(i32)

    top = jnp.where(y == 3, 1, 0)
    some = jnp.where(y >= 1, 1, 0)
    place = meta_of(0, 0)
    above = meta_of(top, top)
    below_above = meta_of(some + top, top)
    below_far = meta_of(some + jnp.where(y >= 2, 1, 0), top)
    far = meta_of(jnp.where(y >= 2, 1, 0), 0)
    e0, at, flags, place, above, below_far, below_above, far = lax.optimization_barrier(
        (e0, at, flags, place, above, below_far, below_above, far)
    )
    e0_there = over_core(e0)
    e1 = over_dec(e0, 1)
    a0, b0 = over_y(e0, 1), over_y(e0, 3)
    e0_far, e0_there = lax.optimization_barrier((e0, e0_there))
    c0 = over_y(e0_far, 2)

    def near(z, meta, q, e, x, arrays=(), units=(), state=()):
        n = len(arrays)
        kv = [pltpu.VMEM((2 * len(units) * SEG, 2 * HD), jnp.bfloat16)] if units else []
        return call(
            functools.partial(near_kernel, z, units),
            meta,
            [q, e, x, *arrays, *state],
            [((tok, 2 * HD), jnp.bfloat16)] * (z == 0) + state_types,
            scratch_shapes=[pltpu.VMEM((SEG, 2 * HD), jnp.bfloat16), *kv],
            input_output_aliases={n + 4 + i: i for i in range(len(state))},
        )

    def more(meta, arrays, units, state, last=False):
        n = len(arrays)
        return call(
            functools.partial(next_kernel, n, units, last),
            meta,
            [q, *arrays, *state],
            state_types + [((tok, 2 * HD), jnp.bfloat16)] * last,
            scratch_shapes=[pltpu.VMEM((2 * len(units) * SEG, 2 * HD), jnp.bfloat16)],
            input_output_aliases={n + 2 + i: i for i in range(4)},
        )

    def both(first, second):
        return over_core(jnp.concatenate([first, second], axis=0))

    pair = [((0, 0),), ((1, 0),)]
    crossed = [((0, 0), (2, SEG)), ((2, 0),)]
    q, *state = near(0, place, queries, e0, e0_there)
    state = more(above, [a0, b0], [pair], state)
    a0, b0, c0, e1, state = lax.optimization_barrier((a0, b0, c0, e1, state))
    ab0_there = both(a0, b0)
    a1, b1 = over_y(e1, 1), over_y(e1, 3)
    e1_there, c0_there = over_core(e1), over_core(c0)
    e1_there, c0_there, state = lax.optimization_barrier((e1_there, c0_there, state))
    distant = [((3, 0),), ((4, 0),)]
    state = near(
        1,
        below_far,
        q,
        e1,
        e1_there,
        [a0, b0, ab0_there, c0, c0_there],
        [crossed, distant],
        state,
    )
    a1, b1, state = lax.optimization_barrier((a1, b1, state))
    ab1_there = both(a1, b1)
    half = SEG // 2
    c1 = over_y(a1[:half], 1), over_y(b1[half:], 3)
    state = more(below_above, [a1, b1, ab1_there], [crossed, pair], state)
    c1, state = lax.optimization_barrier((c1, state))
    c1 = jnp.concatenate(c1, axis=0)
    c1_there = over_core(c1)

    block = ((2 * PAGE, 2 * HD), jnp.bfloat16)
    at, state = lax.optimization_barrier((at, state))
    mine, to_head = call(
        pick_kernel,
        at,
        [e0, e1, b0, b1, c0, c1, a0, a1, e0_there, e1_there, c0_there, c1_there, ab0_there, ab1_there],
        [block] * 2,
    )
    state, mine = lax.optimization_barrier((state, mine))
    oth = over_dec(to_head, 4)
    *_, attended = more(far, [c1, c1_there], [pair], state, True)
    cache_keys, cache_values, key_scales, value_scales = call(
        cache_kernel,
        flags,
        [mine, oth],
        [block, block, ((2, 2), jnp.float32), ((2, 2), jnp.float32)],
    )
    return attended, cache_keys, cache_values, key_scales, value_scales


def solution(mesh):
    return jax.shard_map(
        body,
        mesh=mesh,
        in_specs=(
            P("blk", ("kvh", "dec")),
            P(("blk", "dec"), "kvh"),
            P(("blk", "dec"), "kvh"),
            P(),
        ),
        out_specs=(
            P("blk", ("kvh", "dec")),
            P(("blk", "dec"), "kvh"),
            P(("blk", "dec"), "kvh"),
            P(("blk", "dec"), "kvh"),
            P(("blk", "dec"), "kvh"),
        ),
        check_vma=False,
    )
```

```python
import functools

import jax
import jax.numpy as jnp
import numpy as np
from jax import lax
from jax.experimental import pallas as pl
from jax.experimental.pallas import tpu as pltpu
from jax.sharding import PartitionSpec as P

HEADS = 64
KVH = 8
HD = 128
PAGE = 128
TQ = 512
TN = 256
TS = 128
SEG = 512
C = float(np.log2(np.e) / np.sqrt(HD))
NEG = -1e30
LIMIT = 80.0
NT = (((1,), (1,)), ((), ()))


def longest(x):
    squares = jnp.dot(
        x * x,
        jnp.ones((HD, HD), jnp.bfloat16),
        preferred_element_type=jnp.float32,
    )
    return jnp.sqrt(jnp.max(squares))


def fast(q_ref, state, h, row, size, k, v, allowed=None):
    acc_ref, shift_ref, total_ref = state[:3]
    q = q_ref[rows_at(row, size), h * HD : (h + 1) * HD]
    r = rows_at(h * q_ref.shape[0] + row, size)
    s = lax.dot_general(q, k, NT, preferred_element_type=jnp.float32)
    p = jnp.exp2(s * C - shift_ref[r])
    if allowed is not None:
        p = jnp.where(allowed, p, 0.0)
    total_ref[r] += jnp.sum(p, axis=1, keepdims=True)
    acc_ref[r] += jnp.dot(p.astype(jnp.bfloat16), v, preferred_element_type=jnp.float32)


def slow(q_ref, state, h, row, size, k, v, allowed=True):
    acc_ref, shift_ref, total_ref = state[:3]
    q = q_ref[rows_at(row, size), h * HD : (h + 1) * HD]
    r = rows_at(h * q_ref.shape[0] + row, size)
    s = C * lax.dot_general(q, k, NT, preferred_element_type=jnp.float32)
    s = jnp.where(allowed, s, NEG)
    total = total_ref[r]
    old = jnp.where(total > 0, shift_ref[r], NEG)
    shift = jnp.maximum(old, jnp.max(s, axis=1, keepdims=True))
    p = jnp.where(allowed, jnp.exp2(s - shift), 0.0)
    a = jnp.exp2(old - shift)
    total = a * total + jnp.sum(p, axis=1, keepdims=True)
    shift_ref[r] = jnp.where(total > 0, shift, 0.0)
    total_ref[r] = total
    acc_ref[r] = a * acc_ref[r] + jnp.dot(
        p.astype(jnp.bfloat16), v, preferred_element_type=jnp.float32
    )


def loop(begin, end, step):
    def one(i, _):
        step(i)
        return 0

    lax.fori_loop(begin, end, one, 0)


def rows_at(start, size):
    return pl.ds(start if isinstance(start, int) else pl.multiple_of(start, size), size)


def guarded(state, key_norm, quick, careful):
    shift_ref, bound_ref = state[1], state[3]
    top = jnp.max(bound_ref[:, 0:1]) * key_norm * (1.02 * C) - jnp.min(bound_ref[:, 1:2])

    @pl.when(top <= LIMIT)
    def _():
        quick()

    @pl.when(jnp.logical_not(top <= LIMIT))
    def _():
        careful()
        lowest = jnp.minimum(jnp.min(shift_ref[...]), 0.0)
        bound_ref[:, 1:2] = jnp.full((8, 1), lowest)


def fill(meta, arrays, kv_ref, units):
    for u, unit in enumerate(units):
        for j, choices in enumerate(unit):
            for use, (i, row) in enumerate(choices):
                wanted = meta[0] > u
                if len(choices) > 1:
                    wanted = jnp.logical_and(wanted, meta[1] == use)

                @pl.when(wanted)
                def _():
                    at = (2 * u + j) * SEG
                    kv_ref[at : at + SEG] = arrays[i][row : row + SEG]


def norm_of(kv_ref, count):
    norms = [longest(kv_ref[at : at + 2 * SEG, :HD]) for at in range(0, kv_ref.shape[0], 2 * SEG)]
    norm = jnp.where(count > 0, norms[0], 0.0)
    for u in range(1, len(norms)):
        norm = jnp.maximum(norm, jnp.where(count > u, norms[u], 0.0))
    return norm


def units_quick(q_ref, state, kv_ref, count, finish=None):
    tiles = q_ref.shape[0] // (4 * TN)

    def step(i):
        keys = rows_at((i // tiles) * 2 * SEG, 2 * SEG)
        for part in range(4):
            row = (i % tiles) * 4 * TN + part * TN
            for h in range(2):
                fast(q_ref, state, h, row, TN, kv_ref[keys, :HD], kv_ref[keys, HD:])
                if finish is not None:
                    finish(h, row, TN)

    loop(0, count * tiles, step)


def units_careful(q_ref, state, kv_ref, count):
    few = q_ref.shape[0] // TS

    def step(i):
        keys = rows_at((i // few) * SEG, SEG)
        for h in range(2):
            slow(q_ref, state, h, (i % few) * TS, TS, kv_ref[keys, :HD], kv_ref[keys, HD:])

    loop(0, 2 * count * few, step)


def near_kernel(z, units, meta, q_ref, e_ref, x_ref, *refs):
    count = 0
    if units:
        kv_ref, arrays = refs[-1], refs[: len(refs) - 10]
        refs = refs[:-1]
        count = meta[0]
        fill(meta, arrays, kv_ref, units)
    state, page_ref = refs[-5:-1], refs[-1]
    acc_ref, shift_ref, total_ref, bound_ref = state
    rows = q_ref.shape[0]
    core, dec = meta[2], meta[3]
    if z == 0:
        refs[0][...] = q_ref[...]
        acc_ref[...] = jnp.zeros_like(acc_ref)
        shift_ref[...] = jnp.zeros_like(shift_ref)
        total_ref[...] = jnp.zeros_like(total_ref)
        bound_ref[...] = jnp.zeros_like(bound_ref)
        norm = jnp.maximum(longest(q_ref[:, :HD]), longest(q_ref[:, HD:]))
        bound_ref[:, 0:1] = jnp.full((8, 1), norm)
    parity = jnp.bitwise_xor(dec % 2, z)
    for i in range(SEG // PAGE):
        to = jnp.bitwise_xor(dec // 2, i) * PAGE
        page_ref[rows_at(to, PAGE)] = e_ref[i * PAGE : (i + 1) * PAGE]

    def quick():
        row = lax.broadcasted_iota(jnp.int32, (2 * PAGE, PAGE), 0)
        lane = lax.broadcasted_iota(jnp.int32, (2 * PAGE, PAGE), 1)
        last = parity * PAGE + lane <= row
        for t in range(SEG // PAGE):
            n = (t + 1) * PAGE
            allowed = last
            if t:
                allowed = jnp.concatenate([jnp.full((2 * PAGE, t * PAGE), True), last], axis=1)
            for h in range(2):
                fast(
                    q_ref,
                    state,
                    h,
                    t * 2 * PAGE,
                    2 * PAGE,
                    page_ref[:n, :HD],
                    page_ref[:n, HD:],
                    allowed,
                )

        @pl.when(core == 1)
        def _():
            for row in range(0, rows, TQ):
                for h in range(2):
                    fast(q_ref, state, h, row, TQ, x_ref[:, :HD], x_ref[:, HD:])

        if units:
            units_quick(q_ref, state, kv_ref, count)

    def careful():
        lane = lax.broadcasted_iota(jnp.int32, (1, SEG), 1)
        key_at = (2 * (lane // PAGE) + parity) * PAGE + lane % PAGE

        def diagonal(i):
            allowed = key_at <= i * TS + lax.broadcasted_iota(jnp.int32, (TS, 1), 0)
            for h in range(2):
                slow(q_ref, state, h, i * TS, TS, page_ref[:, :HD], page_ref[:, HD:], allowed)

        def extra(i):
            for h in range(2):
                slow(q_ref, state, h, i * TS, TS, x_ref[:, :HD], x_ref[:, HD:])

        loop(0, rows // TS, diagonal)
        loop(0, jnp.where(core == 1, rows // TS, 0), extra)
        if units:
            units_careful(q_ref, state, kv_ref, count)

    key_norm = jnp.maximum(longest(e_ref[:, :HD]), longest(x_ref[:, :HD]))
    if units:
        key_norm = jnp.maximum(key_norm, norm_of(kv_ref, count))
    guarded(state, key_norm, quick, careful)


def next_kernel(n, units, last, meta, q_ref, *refs):
    arrays = refs[:n]
    if last:
        state, out_ref, kv_ref = refs[-6:-2], *refs[-2:]
    else:
        state, kv_ref = refs[-5:-1], refs[-1]
    rows = q_ref.shape[0]
    count = meta[0]

    def finish(h, row, size):
        r = rows_at(h * rows + row, size)
        mean = state[0][r] * (1.0 / state[2][r])
        out_ref[rows_at(row, size), h * HD : (h + 1) * HD] = mean.astype(jnp.bfloat16)

    def finish_all():
        def step(i):
            for h in range(2):
                finish(h, i * TN, TN)

        loop(0, rows // TN, step)

    def careful():
        units_careful(q_ref, state, kv_ref, count)
        if last:
            finish_all()

    @pl.when(count > 0)
    def _():
        fill(meta, arrays, kv_ref, units)
        guarded(
            state,
            norm_of(kv_ref, count),
            lambda: units_quick(q_ref, state, kv_ref, count, finish if last else None),
            careful,
        )

    if last:
        pl.when(count == 0)(finish_all)


def pick_kernel(meta, *refs):
    pages, outs = refs[:-2], refs[-2:]
    own, (e0, e1, c0, c1, ab0, ab1) = pages[:8], pages[8:]
    places = [(ref, 0) for ref in (*own, e0, e1)]
    places += [(ab0, SEG), (ab1, SEG), (c0, 0), (c1, 0), (ab0, 0), (ab1, 0)]
    def copy(out, j, at):
        for group in range(0, len(places), 4):

            @pl.when(at // 16 == group // 4)
            def _():
                for b in range(group, group + 4):
                    ref, start = places[b]

                    @pl.when(at // 4 == b)
                    def _():
                        rows = rows_at(start + (at % 4) * PAGE, PAGE)
                        out[j * PAGE : (j + 1) * PAGE] = ref[rows]

    for d in range(2):
        for j in range(2):
            copy(outs[d], j, meta[2 * d + j])


def cache_kernel(meta, own, oth, ck, cv, ks, vs):
    col = meta[0]
    scales = [jnp.zeros((2, 2), jnp.float32)] * 2
    row_at = lax.broadcasted_iota(jnp.int32, (2, 2), 0)
    col_at = lax.broadcasted_iota(jnp.int32, (2, 2), 1)
    for j in range(2):
        filled = meta[1 + j] > 0
        rows = slice(j * PAGE, (j + 1) * PAGE)
        for kind, out in enumerate((ck, cv)):
            normed = []
            for b, block in enumerate((own, oth)):
                x = block[rows, kind * HD : (kind + 1) * HD].astype(jnp.float32)
                x = jnp.where(filled, x, 0.0)
                scale = jnp.max(jnp.abs(x), keepdims=True) + 1e-6
                normed.append((x / scale).astype(jnp.bfloat16))
                here = jnp.logical_and(row_at == j, col_at == (col if b == 0 else 1 - col))
                scales[kind] = jnp.where(jnp.logical_and(here, filled), scale, scales[kind])
            out[rows, :HD] = jnp.where(col == 0, normed[0], normed[1])
            out[rows, HD:] = jnp.where(col == 0, normed[1], normed[0])
    ks[...] = scales[0]
    vs[...] = scales[1]


VMEM = pl.BlockSpec(memory_space=pltpu.VMEM)
SMEM = pl.BlockSpec(memory_space=pltpu.SMEM)
PARAMS = pltpu.CompilerParams(vmem_limit_bytes=10 * 2**20)


def call(kernel, meta, arrays, outs, **more):
    return pl.pallas_call(
        kernel,
        in_specs=[SMEM] + [VMEM] * len(arrays),
        out_specs=[VMEM] * len(outs),
        out_shape=[jax.ShapeDtypeStruct(s, t) for s, t in outs],
        compiler_params=PARAMS,
        **more,
    )(meta, *arrays)


def body(queries, keys, values, page_slot):
    blk, dec = lax.axis_index("blk"), lax.axis_index("dec")
    y, core, head = blk // 2, blk % 2, dec // 4
    tok = queries.shape[0]
    i32 = jnp.int32

    def over_dec(x, m):
        return lax.ppermute(x, "dec", [(i, i ^ m) for i in range(8)])

    def over_core(x):
        return lax.ppermute(x, "blk", [(i, i ^ 1) for i in range(8)])

    def over_y(x, d):
        return lax.ppermute(x, "blk", [(i, (i + 2 * d) % 8) for i in range(8)])

    first = jnp.concatenate([keys[:, :HD], values[:, :HD]], axis=1)
    second = jnp.concatenate([keys[:, HD:], values[:, HD:]], axis=1)
    own = jnp.where(head == 0, first, second)
    other = jnp.where(head == 0, second, first)

    e0 = jnp.concatenate(
        [own, over_dec(own, 2), over_dec(other, 4), over_dec(other, 6)], axis=0
    )

    owners = jnp.stack([8 * blk + dec, 8 * blk + (dec ^ 4)])
    slots = (2 * owners[:, None] + jnp.arange(2)[None, :]).reshape(4)
    hits = page_slot[None, :] == slots[:, None]
    filled = jnp.any(hits, axis=1)
    page = jnp.sum(jnp.where(hits, jnp.arange(64)[None, :], 0), axis=1)
    page_blk, page_dec = page // 8, page % 8
    rel = page_dec ^ dec
    buffer = 8 * ((page_blk % 2) ^ core) + 2 * ((page_blk // 2 - y) % 4) + rel % 2
    at = jnp.where(filled, 4 * buffer + rel // 2, -1).astype(i32)
    flags = jnp.concatenate([head[None], filled[:2]]).astype(i32)

    state_types = [
        ((2 * tok, HD), jnp.float32),
        ((2 * tok, 1), jnp.float32),
        ((2 * tok, 1), jnp.float32),
        ((8, 2), jnp.float32),
    ]
    def meta_of(count, other):
        return jnp.stack([count + 0 * y, other + 0 * y, core, dec]).astype(i32)

    top = jnp.where(y == 3, 1, 0)
    some = jnp.where(y >= 1, 1, 0)
    place = meta_of(0, 0)
    above = meta_of(top, top)
    below_above = meta_of(some + top, top)
    below_far = meta_of(some + jnp.where(y >= 2, 1, 0), top)
    far = meta_of(jnp.where(y >= 2, 1, 0), 0)
    e0, at, flags, place, above, below_far, below_above, far = lax.optimization_barrier(
        (e0, at, flags, place, above, below_far, below_above, far)
    )
    e0_there = over_core(e0)
    e1 = over_dec(e0, 1)
    a0, b0 = over_y(e0, 1), over_y(e0, 3)
    e0_far, e0_there = lax.optimization_barrier((e0, e0_there))
    c0 = over_y(e0_far, 2)

    def near(z, meta, q, e, x, arrays=(), units=(), state=()):
        n = len(arrays)
        kv = [pltpu.VMEM((2 * len(units) * SEG, 2 * HD), jnp.bfloat16)] if units else []
        return call(
            functools.partial(near_kernel, z, units),
            meta,
            [q, e, x, *arrays, *state],
            [((tok, 2 * HD), jnp.bfloat16)] * (z == 0) + state_types,
            scratch_shapes=[pltpu.VMEM((SEG, 2 * HD), jnp.bfloat16), *kv],
            input_output_aliases={n + 4 + i: i for i in range(len(state))},
        )

    def more(meta, arrays, units, state, last=False):
        n = len(arrays)
        return call(
            functools.partial(next_kernel, n, units, last),
            meta,
            [q, *arrays, *state],
            state_types + [((tok, 2 * HD), jnp.bfloat16)] * last,
            scratch_shapes=[pltpu.VMEM((2 * len(units) * SEG, 2 * HD), jnp.bfloat16)],
            input_output_aliases={n + 2 + i: i for i in range(4)},
        )

    def both(first, second):
        return over_core(jnp.concatenate([first, second], axis=0))

    pair = [((0, 0),), ((1, 0),)]
    crossed = [((0, 0), (2, SEG)), ((2, 0),)]
    q, *state = near(0, place, queries, e0, e0_there)
    state = more(above, [a0, b0], [pair], state)
    a0, b0, c0, e1, state = lax.optimization_barrier((a0, b0, c0, e1, state))
    ab0_there = both(a0, b0)
    a1, b1 = over_y(e1, 1), over_y(e1, 3)
    e1_there, c0_there = over_core(e1), over_core(c0)
    e1_there, c0_there, state = lax.optimization_barrier((e1_there, c0_there, state))
    distant = [((3, 0),), ((4, 0),)]
    state = near(
        1,
        below_far,
        q,
        e1,
        e1_there,
        [a0, b0, ab0_there, c0, c0_there],
        [crossed, distant],
        state,
    )
    a1, b1, state = lax.optimization_barrier((a1, b1, state))
    ab1_there = both(a1, b1)
    half = SEG // 2
    c1 = over_y(a1[:half], 1), over_y(b1[half:], 3)
    state = more(below_above, [a1, b1, ab1_there], [crossed, pair], state)
    c1, state = lax.optimization_barrier((c1, state))
    c1 = jnp.concatenate(c1, axis=0)
    c1_there = over_core(c1)

    block = ((2 * PAGE, 2 * HD), jnp.bfloat16)
    at, state = lax.optimization_barrier((at, state))
    mine, to_head = call(
        pick_kernel,
        at,
        [e0, e1, b0, b1, c0, c1, a0, a1, e0_there, e1_there, c0_there, c1_there, ab0_there, ab1_there],
        [block] * 2,
    )
    state, mine = lax.optimization_barrier((state, mine))
    oth = over_dec(to_head, 4)
    *_, attended = more(far, [c1, c1_there], [pair], state, True)
    cache_keys, cache_values, key_scales, value_scales = call(
        cache_kernel,
        flags,
        [mine, oth],
        [block, block, ((2, 2), jnp.float32), ((2, 2), jnp.float32)],
    )
    return attended, cache_keys, cache_values, key_scales, value_scales


def solution(mesh):
    return jax.shard_map(
        body,
        mesh=mesh,
        in_specs=(
            P("blk", ("kvh", "dec")),
            P(("blk", "dec"), "kvh"),
            P(("blk", "dec"), "kvh"),
            P(),
        ),
        out_specs=(
            P("blk", ("kvh", "dec")),
            P(("blk", "dec"), "kvh"),
            P(("blk", "dec"), "kvh"),
            P(("blk", "dec"), "kvh"),
            P(("blk", "dec"), "kvh"),
        ),
        check_vma=False,
    )
```
